512 devices in a mesh: range: 32 (over x, z_lo), height: 16 (over y, z_hi, core).
Axes of the slice: x: 4, y: 4, z: 16 (z_hi: 2, z_lo: 8; z = z_hi * 8 + z_lo), core: 2. Of those that a mesh axis runs over, the one named last changes fastest.
Arguments:
- pressure: float32 [1536, 128, 128], P('range', 'height'), may hold values from -6 to 6
- vertical_flow: float32 [1536, 128, 128], P('range', 'height'), may hold values from -6 to 6
- radial_flow: float32 [1536, 128, 128], P('range', 'height'), may hold values from -6 to 6
- lateral_flow: float32 [1536, 128, 128], P('range', 'height'), may hold values from -6 to 6
- stiffness: float32 [128, 128], P('height'), may hold values from 0.3 to 0.8
- buoyancy: float32 [128, 128], P('height'), may hold values from 0.12 to 0.25
- wind_profile: float32 [128], replicated, may hold values from -0.15 to 0.15
Outputs:
- final_pressure: float32 [1536, 128, 128], P('range', 'height')
- final_vertical: float32 [1536, 128, 128], P('range', 'height')
- final_radial: float32 [1536, 128, 128], P('range', 'height')
- final_lateral: float32 [1536, 128, 128], P('range', 'height')
The draws below stay inside these ranges and needn't reach their ends.
All inputs are finite; a program needn't handle non-finite values.
Results may differ from the reference program's by a relative error of at most 0.00002.
Values sent between devices are 32-bit elements; how exact they have to be, the bound alone decides.
A program may use at most 64 MiB of HBM per device.

```python
import math
import jax
import jax.numpy as jnp
from jax import lax

LAT = 128
SHIFT = 8
STEPS = 2
NR = 1536
NH = 128


def draw_pressure(key, part):
    key = jax.random.fold_in(key, 11)
    rough = jax.random.normal(key, (NR, NH, LAT), jnp.float32)
    field = rough
    return jnp.clip(field, -6.0, 6.0)


def steps_of(key, shape, split, smallest, top_value):
    level = 1.0
    for position, blocks in split:
        heights = jax.random.uniform(jax.random.fold_in(jax.random.fold_in(key, 6), position), (blocks,), jnp.float32, smallest / len(split), top_value / len(split))
        level = level * jnp.repeat(jnp.exp(heights), shape[position] // blocks).reshape((-1,) + (1,) * (len(shape) - 1 - position))
    return level


def gaussian(key, dims, width, reach, split=(), held_as=jnp.bfloat16):
    array = jax.random.normal(key, dims, jnp.float32) * width
    if len(split) > 0:
        array = steps_of(key, dims, split, -0.22, 0.18) * array
    return jnp.clip(array, min=-reach, max=reach).astype(held_as)


def setup_inputs(seed: int = 0) -> dict:
    arg_keys = jax.random.split(jax.random.key(seed), 8)
    pressure = draw_pressure(jax.random.fold_in(arg_keys[7], 71), 0)
    vertical_flow = gaussian(arg_keys[1], (NR, NH, LAT), 1.0, 6.0, ((0, 32), (1, 16)), jnp.float32)
    radial_flow = gaussian(arg_keys[2], (NR, NH, LAT), 1.0, 6.0, ((0, 32), (1, 16)), jnp.float32)
    lateral_flow = gaussian(arg_keys[3], (NR, NH, LAT), 1.0, 6.0, ((0, 32), (1, 16)), jnp.float32)
    stiffness = jnp.clip(jnp.exp(math.log(0.8) - 0.98082923 * jax.random.uniform(arg_keys[4], (NH, LAT), jnp.float32) ** steps_of(arg_keys[4], (NH, LAT), ((0, 16),), -0.2, 0.2)), 0.3, 0.8)
    buoyancy = jnp.clip(jnp.exp(math.log(0.25) - 0.7339692 * jax.random.uniform(arg_keys[5], (NH, LAT), jnp.float32) ** steps_of(arg_keys[5], (NH, LAT), ((0, 16),), -0.2, 0.2)), 0.12, 0.25)
    wind_profile = jnp.clip(jax.random.uniform(arg_keys[6], (NH,), jnp.float32, -0.15, 0.15), -0.15, 0.15)
    return {"pressure": pressure, "vertical_flow": vertical_flow, "radial_flow": radial_flow, "lateral_flow": lateral_flow, "stiffness": stiffness, "buoyancy": buoyancy, "wind_profile": wind_profile}


def pad_axis(field, axis):
    widths = [(0, 0)] * field.ndim
    widths[axis] = (2, 2)
    return jnp.pad(field, widths)


def piece(padded, start, count, axis):
    return lax.slice_in_dim(padded, start, start + count, axis=axis)


def forward_diff(padded, axis, count):
    return (27.0 * (piece(padded, 3, count, axis) - piece(padded, 2, count, axis)) - (piece(padded, 4, count, axis) - piece(padded, 1, count, axis))) / 24.0


def backward_diff(padded, axis, count):
    return (27.0 * (piece(padded, 2, count, axis) - piece(padded, 1, count, axis)) - (piece(padded, 3, count, axis) - piece(padded, 0, count, axis))) / 24.0


def central_diff(padded, axis, count):
    return (8.0 * (piece(padded, 3, count, axis) - piece(padded, 1, count, axis)) - (piece(padded, 4, count, axis) - piece(padded, 0, count, axis))) / 12.0


def lateral_forward(field):
    return (27.0 * (jnp.roll(field, -1, -1) - field) - (jnp.roll(field, -2, -1) - jnp.roll(field, 1, -1))) / 24.0


def lateral_backward(field):
    return (27.0 * (field - jnp.roll(field, 1, -1)) - (jnp.roll(field, -1, -1) - jnp.roll(field, 2, -1))) / 24.0


def lateral_central(field):
    return (8.0 * (jnp.roll(field, -1, -1) - jnp.roll(field, 1, -1)) - (jnp.roll(field, -2, -1) - jnp.roll(field, 2, -1))) / 12.0


def advance(press, vert, radial, lateral, stiff, buoy, advect, shear):
    count_r = press.shape[0]
    count_h = press.shape[1]
    press_r = pad_axis(press, 0)
    press_h = pad_axis(press, 1)
    vert_h = pad_axis(vert, 1)
    radial_new = radial - buoy * forward_diff(press_r, 0, count_r) - advect * central_diff(pad_axis(radial, 0), 0, count_r) - shear * 0.5 * (piece(vert_h, 2, count_h, 1) + piece(vert_h, 1, count_h, 1))
    lateral_new = lateral - buoy * lateral_forward(press) - advect * central_diff(pad_axis(lateral, 0), 0, count_r)
    vert_new = vert - buoy * forward_diff(press_h, 1, count_h) - advect * central_diff(pad_axis(vert, 0), 0, count_r)
    spread = backward_diff(pad_axis(radial_new, 0), 0, count_r) + lateral_backward(lateral_new) + backward_diff(pad_axis(vert_new, 1), 1, count_h)
    press_new = press - stiff * spread - advect * central_diff(press_r, 0, count_r)
    return press_new, vert_new, radial_new, lateral_new


def advance_frame(field):
    tail = jnp.zeros((SHIFT,) + field.shape[1:], jnp.float32)
    return jnp.concatenate([field[SHIFT:], tail], axis=0)


def reference(pressure, vertical_flow, radial_flow, lateral_flow, stiffness, buoyancy, wind_profile):
    edged = jnp.concatenate([wind_profile[:1], wind_profile, wind_profile[-1:]])
    shear = (0.5 * (edged[2:] - edged[:-2]))[None, :, None]
    advect = wind_profile[None, :, None]
    stiff = stiffness[None]
    buoy = buoyancy[None]
    press, vert, radial, lateral = pressure, vertical_flow, radial_flow, lateral_flow
    for step in range(STEPS):
        press, vert, radial, lateral = advance(press, vert, radial, lateral, stiff, buoy, advect, shear)
        if step + 1 == STEPS // 2:
            press = advance_frame(press)
            vert = advance_frame(vert)
            radial = advance_frame(radial)
            lateral = advance_frame(lateral)
    return press, vert, radial, lateral
```

```python
import jax
import jax.numpy as jnp
from jax import lax
from jax.experimental import pallas as pl
from jax.experimental.pallas import tpu as pltpu
from jax.sharding import PartitionSpec as P

MESH = pl.DeviceIdType.MESH
N = 48
H = 8
HALO = 14
SHIFT = 8
BASE = 3
ROWS = 56
FIRST = 40
UP, DOWN = 7, 6


def planes(ref, start, count):
    rows = pl.ds(pl.multiple_of(start * H, H), count * H)
    return ref[rows, :].reshape(count, H, 128)


def put(ref, start, value):
    rows = pl.ds(pl.multiple_of(start * H, H), value.shape[0] * H)
    ref[rows, :] = value.reshape(value.shape[0] * H, 128)


def row(ref, start, k):
    return ref[pl.ds(start * H + k, H, stride=H), :]


def put_row(ref, start, k, value):
    ref[pl.ds(start * H + k, H, stride=H), :] = value


def lat(value, steps):
    return pltpu.roll(value, steps % 128, 2)


def hgt(value, steps):
    return pltpu.roll(value, steps % H, 1)


def central(x, count):
    return 8.0 * (x[3 : 3 + count] - x[1 : 1 + count]) - (x[4 : 4 + count] - x[0:count])


def flows(src, dst, start, count, to, coef):
    press, vert, radial, lateral = src
    new_vert, new_radial, new_lateral = dst
    p = planes(press, start - 1, count + 3)
    u = planes(radial, start - 2, count + 4)
    v = planes(lateral, start - 2, count + 4)
    w = planes(vert, start - 2, count + 4)
    b1, a1, s0, s1, k0, k1, k2, km = (coef[i] for i in range(8))
    here, mid = p[1 : 1 + count], w[2 : 2 + count]
    put(
        new_radial,
        to,
        u[2 : 2 + count]
        - b1 * (27.0 * (p[2 : 2 + count] - here) - (p[3 : 3 + count] - p[0:count]))
        - a1 * central(u, count)
        - (s0 * mid + s1 * hgt(mid, 1)),
    )
    put(
        new_lateral,
        to,
        v[2 : 2 + count]
        - b1 * (27.0 * (lat(here, -1) - here) - (lat(here, -2) - lat(here, 1)))
        - a1 * central(v, count),
    )
    put(
        new_vert,
        to,
        mid
        + (k0 * here - k1 * hgt(here, -1))
        + (k2 * hgt(here, -2) - km * hgt(here, 1))
        - a1 * central(w, count),
    )


def pressures(press, new, dst, start, at, count, to, coef):
    new_vert, new_radial, new_lateral = new
    p = planes(press, start - 2, count + 4)
    u = planes(new_radial, at - 2, count + 3)
    v = planes(new_lateral, at, count)
    w = planes(new_vert, at, count)
    c1, a1, d1, d2, dm = coef[8], coef[1], coef[9], coef[10], coef[11]
    spread = (
        27.0 * (u[2 : 2 + count] - u[1 : 1 + count])
        - (u[3 : 3 + count] - u[0:count])
        + 27.0 * (v - lat(v, 1))
        - (lat(v, -1) - lat(v, 2))
        + (27.0 * w - d1 * hgt(w, 1))
        - (dm * hgt(w, -1) - d2 * hgt(w, 2))
    )
    put(dst, to, p[2 : 2 + count] - c1 * spread - a1 * central(p, count))


def kernel(
    ranges,
    heights,
    press_in,
    vert_in,
    radial_in,
    lateral_in,
    stiff_in,
    buoy_in,
    wind_in,
    press_out,
    vert_out,
    radial_out,
    lateral_out,
    p0,
    w0,
    u0,
    v0,
    p1,
    w1,
    u1,
    v1,
    p2,
    w2,
    u2,
    v2,
    stiff,
    buoy,
    wind,
    coef,
    up_send,
    up_recv,
    down_send,
    down_recv,
    up_more,
    low_more,
    down_more,
    high_more,
    low_w,
    halo,
    local_sem,
    send_sem,
    recv_sem,
):
    r, h = lax.axis_index("range"), lax.axis_index("height")
    first_r, last_r = r == 0, r == ranges - 1
    first_h, last_h = h == 0, h == heights - 1
    left = (lax.rem(r + ranges - 1, ranges), h)
    right = (lax.rem(r + 1, ranges), h)
    below = (r, lax.rem(h + heights - 1, heights))
    above = (r, lax.rem(h + 1, heights))
    no_left, no_right = jnp.logical_not(first_r), jnp.logical_not(last_r)
    no_below, no_above = jnp.logical_not(first_h), jnp.logical_not(last_h)

    barrier = pltpu.get_barrier_semaphore()
    for there, device in ((no_below, below), (no_above, above), (no_right, right)):

        @pl.when(there)
        def _():
            pl.semaphore_signal(barrier, inc=1, device_id=device, device_id_type=MESH)

    whole = pl.ds(0, N * H)
    loads = [
        pltpu.make_async_copy(src, dst, local_sem.at[i])
        for i, (src, dst) in enumerate(
            (
                (buoy_in, buoy),
                (stiff_in, stiff),
                (wind_in, wind),
                (press_in, p0.at[whole]),
                (vert_in, w0.at[whole]),
                (radial_in, u0.at[whole]),
                (lateral_in, v0.at[whole]),
            )
        )
    ]
    for load in loads:
        load.start()
    for load in loads[:3]:
        load.wait()

    k = lax.broadcasted_iota(jnp.int32, (H, 128), 0)
    lane = lax.broadcasted_iota(jnp.int32, (H, 128), 1)
    spread_wind = jnp.broadcast_to(wind[...], (H, 128))
    top = heights * H - 1

    def wind_at(rows):
        chosen = jnp.where(lane == rows, spread_wind, 0.0)
        return jnp.broadcast_to(jnp.sum(chosen, axis=1, keepdims=True), (H, 128))

    def shear_at(rows):
        upper = wind_at(jnp.where(rows < top, rows + 1, top))
        lower = wind_at(jnp.where(rows > 0, rows - 1, 0))
        return 0.5 * (upper - lower)

    mine = k + h * H
    b24, c24 = buoy[...] * (1.0 / 24.0), stiff[...] * (1.0 / 24.0)
    a12 = wind_at(mine) * (1.0 / 12.0)
    half_shear = 0.5 * shear_at(mine)
    b27 = b24 * 27.0
    full = jnp.full((H, 128), 27.0, jnp.float32)
    one = jnp.full((H, 128), 1.0, jnp.float32)
    for i, value in enumerate(
        (
            b24,
            a12,
            half_shear,
            jnp.where(k > 0, half_shear, 0.0),
            b27,
            jnp.where(k < H - 1, b27, 0.0),
            jnp.where(k < H - 2, b24, 0.0),
            jnp.where(k > 0, b24, 0.0),
            c24,
            jnp.where(k > 0, full, 0.0),
            jnp.where(k > 1, one, 0.0),
            jnp.where(k < H - 1, one, 0.0),
        )
    ):
        coef[i] = value
    a_low1 = wind_at(jnp.full((H, 128), -1, jnp.int32) + h * H) * (1.0 / 12.0)
    a_low2 = wind_at(jnp.full((H, 128), -2, jnp.int32) + h * H) * (1.0 / 12.0)
    a_high = wind_at(jnp.full((H, 128), 8, jnp.int32) + h * H) * (1.0 / 12.0)
    s_high = 0.5 * shear_at(jnp.full((H, 128), 8, jnp.int32) + h * H)
    s_low = 0.5 * shear_at(jnp.full((H, 128), 0, jnp.int32) + h * H)

    up_more[pl.ds(0, H), :] = b24
    down_more[pl.ds(0, H), :] = b24
    up_more[pl.ds(H, H), :] = c24
    down_more[pl.ds(H, H), :] = c24

    def free_flows(start, step, times):
        def body(j, carry):
            at = start + step * j
            flows((p0, w0, u0, v0), (w1, u1, v1), at, step, at, coef)
            return carry

        lax.fori_loop(0, times, body, 0)

    def free_pressures(start, step, times):
        def body(j, carry):
            at = start + step * j
            pressures(p0, (w1, u1, v1), p1, at, at, step, at, coef)
            return carry

        lax.fori_loop(0, times, body, 0)

    def pack(first, last):
        def body(j, carry):
            at = BASE + H * j
            to = pl.ds(pl.multiple_of(j * H, H), H)
            for q, (ref, height) in enumerate(
                ((p0, 7), (w0, 7), (w1, 7), (w1, 6), (p1, 7), (p1, 6), (p1, 5))
            ):
                up_send[q, to, :] = row(ref, at, height)
            for q, (ref, height) in enumerate(
                ((p0, 0), (p0, 1), (w1, 0), (p1, 0), (p1, 1), (p1, 2))
            ):
                down_send[q, to, :] = row(ref, at, height)
            return carry

        lax.fori_loop(first, last, body, 0)

    def remote(src, dst, i, device):
        return pltpu.make_async_remote_copy(
            src_ref=src,
            dst_ref=dst,
            send_sem=send_sem.at[i],
            recv_sem=recv_sem.at[i],
            device_id=device,
            device_id_type=MESH,
        )

    early, late = pl.ds(0, FIRST), pl.ds(FIRST, ROWS - FIRST)
    head, tail = pl.ds(0, HALO * H), pl.ds(N * H, HALO * H)
    ups = [
        remote(up_send.at[:, early], up_recv.at[:, early], 0, above),
        remote(up_send.at[:, late], up_recv.at[:, late], 1, above),
        remote(up_more, low_more, 2, above),
    ]
    downs = [
        remote(down_send.at[:, early], down_recv.at[:, early], 3, below),
        remote(down_send.at[:, late], down_recv.at[:, late], 4, below),
        remote(down_more, high_more, 5, below),
    ]
    lefts = [
        remote(src.at[head], dst.at[tail], 6 + i, left)
        for i, (src, dst) in enumerate(
            ((press_in, p0), (radial_in, u0), (vert_in, w0), (lateral_in, v0))
        )
    ]

    for load in loads[3:]:
        load.wait()
    free_flows(BASE, 6, 7)
    free_pressures(BASE, 5, 8)
    pack(0, FIRST // H)

    peers = sum(there.astype(jnp.int32) for there in (no_below, no_above, no_left))
    pl.semaphore_wait(barrier, peers)

    pl.when(no_above)(ups[0].start)
    pl.when(no_below)(downs[0].start)

    @pl.when(no_left)
    def _():
        for copy in lefts:
            copy.start()

    nothing = jnp.zeros((HALO * H, 128), jnp.float32)

    @pl.when(last_r)
    def _():
        for ref in (p0, u0, w0, v0):
            ref[tail, :] = nothing

    @pl.when(no_right)
    def _():
        for copy in lefts:
            copy.wait_recv()

    free_flows(45, 5, 3)

    def clear_after():
        for ref in (u1, v1, w1, p1):
            ref[pl.ds(N * H, 12 * H), :] = jnp.zeros((12 * H, 128), jnp.float32)

    pl.when(last_r)(clear_after)
    free_pressures(43, 4, 4)
    pl.when(last_r)(clear_after)
    pack(FIRST // H, ROWS // H)
    last = row(w0, BASE + ROWS - H + 1, 7)
    up_more[pl.ds(2 * H, H), :] = last

    @pl.when(no_above)
    def _():
        ups[1].start()
        ups[2].start()

    @pl.when(no_below)
    def _():
        downs[1].start()
        downs[2].start()

    @pl.when(no_below)
    def _():
        for copy in ups:
            copy.wait_recv()

    @pl.when(no_above)
    def _():
        for copy in downs:
            copy.wait_recv()

    @pl.when(first_h)
    def _():
        up_recv[...] = jnp.zeros(up_recv.shape, jnp.float32)
        low_more[...] = jnp.zeros(low_more.shape, jnp.float32)

    @pl.when(last_h)
    def _():
        down_recv[...] = jnp.zeros(down_recv.shape, jnp.float32)
        high_more[...] = jnp.zeros(high_more.shape, jnp.float32)

    def line(ref, i):
        return jnp.broadcast_to(ref[pl.ds(i, 1), :], (H, 128))

    def own(ref, i):
        return jnp.broadcast_to(ref[i : i + 1, :], (H, 128))

    low_w[pl.ds(0, H), :] = jnp.zeros((H, 128), jnp.float32)
    low_w[pl.ds(H, ROWS), :] = up_recv[1]
    low_w[pl.ds(H + ROWS, H), :] = jnp.broadcast_to(
        low_more[pl.ds(3 * H - 1, 1), :], (H, 128)
    )
    first_plane = jnp.where(first_r, SHIFT, 0)
    after_plane = jnp.where(last_r, N, 2 * N)

    def changes(low_p, low_w, high_p, high_p2):
        d0 = own(b24, 0) * low_p * -1.0
        d7 = own(b24, 7) * (high_p2 - 27.0 * high_p)
        d6 = own(b24, 6) * high_p
        return d0, d6, d7

    def correct_pressure(ref, at, du, d0, d6, d7, low1, low2, high):
        for i, add in (
            (0, du + 27.0 * (d0 - low1) + low2),
            (1, low1 - 27.0 * d0),
            (2, d0),
            (5, -d6),
            (6, 27.0 * d6 - d7),
            (7, 27.0 * (d7 - d6) - high),
        ):
            put_row(ref, at, i, row(ref, at, i) - own(c24, i) * add)

    def correct_first(j, carry):
        at = BASE + H * j
        here = pl.ds(pl.multiple_of(j * H, H), H)
        low_p0, low_w1, low_w2 = up_recv[0, here, :], up_recv[2, here, :], up_recv[3, here, :]
        high_p0, high_p0b = down_recv[0, here, :], down_recv[1, here, :]
        wl = [low_w[pl.ds(j * H + H + s, H), :] for s in (-2, -1, 0, 1)]
        wt = [row(w0, at + s, 7) for s in (-2, -1, 0, 1)]
        own_p0, own_p1, own_p7 = row(p0, at, 0), row(p0, at, 1), row(p0, at, 7)
        e1 = line(low_more, 7) * (own_p1 - 27.0 * own_p0)
        e2 = line(low_more, 6) * own_p0
        e8 = line(high_more, 0) * own_p7 * -1.0
        low_w1, low_w2 = low_w1 + e1, low_w2 + e2
        high_w = down_recv[2, here, :] + e8
        d0, d6, d7 = changes(low_p0, None, high_p0, high_p0b)
        new0, new6, new7 = row(w1, at, 0) + d0, row(w1, at, 6) + d6, row(w1, at, 7) + d7
        put_row(w1, at, 0, new0)
        put_row(w1, at, 6, new6)
        put_row(w1, at, 7, new7)
        put_row(u1, at, 0, row(u1, at, 0) - s_low * wl[2])
        du = -s_low * (27.0 * (wl[2] - wl[1]) - (wl[3] - wl[0]))
        correct_pressure(p1, at, du, d0, d6, d7, low_w1, low_w2, high_w)
        du_high = -s_high * (27.0 * (wt[2] - wt[1]) - (wt[3] - wt[0]))
        low_p1 = up_recv[4, here, :] - line(low_more, H + 7) * (27.0 * (e1 - e2) - new0)
        low_p2 = up_recv[5, here, :] - line(low_more, H + 6) * (27.0 * e2 - e1)
        low_p3 = up_recv[6, here, :] + line(low_more, H + 5) * e2
        high_p1 = down_recv[3, here, :] - line(high_more, H) * (
            du_high + 27.0 * (e8 - new7) + new6
        )
        high_p2 = down_recv[4, here, :] - line(high_more, H + 1) * (new7 - 27.0 * e8)
        high_p3 = down_recv[5, here, :] - line(high_more, H + 2) * e8
        plane = k + at
        keep = jnp.logical_and(plane >= first_plane, plane < after_plane)
        for i, value in enumerate(
            (low_w1, low_w2, low_p1, low_p2, low_p3, high_w, high_p1, high_p2, high_p3)
        ):
            halo[i, here, :] = jnp.where(keep, value, 0.0)
        return carry

    lax.fori_loop(0, ROWS // H, correct_first, 0)

    @pl.when(first_r)
    def _():
        for ref in (u1, v1, w1, p1):
            ref[pl.ds(0, SHIFT * H), :] = jnp.zeros((SHIFT * H, 128), jnp.float32)

    pl.when(last_r)(clear_after)

    def second_flows(j, carry):
        at = 8 * j
        flows((p1, w1, u1, v1), (w2, u2, v2), at + SHIFT, 8, at + 2, coef)
        return carry

    lax.fori_loop(0, N // 8, second_flows, 0)
    flows((p1, w1, u1, v1), (w2, u2, v2), SHIFT - 2, 2, 0, coef)
    flows((p1, w1, u1, v1), (w2, u2, v2), SHIFT + N, 1, N + 2, coef)

    @pl.when(first_r)
    def _():
        u2[pl.ds(0, 2 * H), :] = jnp.zeros((2 * H, 128), jnp.float32)

    def second_pressures(j, carry):
        at = 8 * j
        pressures(p1, (w2, u2, v2), p2, at + SHIFT, at + 2, 8, at, coef)
        return carry

    lax.fori_loop(0, N // 8, second_pressures, 0)

    def correct_second(j, carry):
        at = H * j
        off = at + SHIFT - BASE

        def rows_of(i, s=0):
            return halo[i, pl.ds(off + s, H), :]

        def across(i):
            return 8.0 * (rows_of(i, 1) - rows_of(i, -1)) - (rows_of(i, 2) - rows_of(i, -2))

        low_w1, low_w2, low_p1, low_p2, low_p3, high_w, high_p1, high_p2, high_p3 = (
            rows_of(i) for i in range(9)
        )
        own_p0, own_p1, own_p7 = (row(p1, at + SHIFT, i) for i in (0, 1, 7))
        d0, d6, d7 = changes(low_p1, None, high_p1, high_p2)
        put_row(w2, at + 2, 0, row(w2, at + 2, 0) + d0)
        put_row(w2, at + 2, 6, row(w2, at + 2, 6) + d6)
        put_row(w2, at + 2, 7, row(w2, at + 2, 7) + d7)
        put_row(u2, at + 2, 0, row(u2, at + 2, 0) - s_low * low_w1)
        du = -s_low * (
            27.0 * (low_w1 - rows_of(0, -1)) - (rows_of(0, 1) - rows_of(0, -2))
        )
        new1 = (
            low_w1
            - line(low_more, 7) * (27.0 * (own_p0 - low_p1) - (own_p1 - low_p2))
            - a_low1 * across(0)
        )
        new2 = (
            low_w2
            - line(low_more, 6) * (27.0 * (low_p1 - low_p2) - (own_p0 - low_p3))
            - a_low2 * across(1)
        )
        new8 = (
            high_w
            - line(high_more, 0) * (27.0 * (high_p2 - high_p1) - (high_p3 - own_p7))
            - a_high * across(5)
        )
        correct_pressure(p2, at, du, d0, d6, d7, new1, new2, new8)
        return carry

    lax.fori_loop(0, N // H, correct_second, 0)

    inner = pl.ds(2 * H, N * H)
    stores = [
        pltpu.make_async_copy(src, dst, local_sem.at[i])
        for i, (src, dst) in enumerate(
            (
                (p2, press_out),
                (w2.at[inner], vert_out),
                (u2.at[inner], radial_out),
                (v2.at[inner], lateral_out),
            )
        )
    ]
    for store in stores:
        store.start()

    @pl.when(no_above)
    def _():
        for copy in ups:
            copy.wait_send()

    @pl.when(no_below)
    def _():
        for copy in downs:
            copy.wait_send()

    @pl.when(no_left)
    def _():
        for copy in lefts:
            copy.wait_send()

    for store in stores:
        store.wait()


def solution(mesh):
    ranges, heights = mesh.shape["range"], mesh.shape["height"]

    def on_device(press, vert, radial, lateral, stiff, buoy, wind):
        def field(count):
            return pltpu.VMEM((count * H, 128), jnp.float32)

        flat = [x.reshape(N * H, 128) for x in (press, vert, radial, lateral)]
        out = pl.pallas_call(
            lambda *refs: kernel(ranges, heights, *refs),
            out_shape=[jax.ShapeDtypeStruct((N * H, 128), jnp.float32)] * 4,
            in_specs=[pl.BlockSpec(memory_space=pl.ANY)] * 7,
            out_specs=[pl.BlockSpec(memory_space=pl.ANY)] * 4,
            scratch_shapes=[field(64)] * 8
            + [field(N), field(N + 4), field(N + 4), field(N + 4)]
            + [
                field(1),
                field(1),
                pltpu.VMEM((1, 128), jnp.float32),
                pltpu.VMEM((12, H, 128), jnp.float32),
                pltpu.VMEM((UP, ROWS, 128), jnp.float32),
                pltpu.VMEM((UP, ROWS, 128), jnp.float32),
                pltpu.VMEM((DOWN, ROWS, 128), jnp.float32),
                pltpu.VMEM((DOWN, ROWS, 128), jnp.float32),
                field(3),
                field(3),
                field(2),
                field(2),
                pltpu.VMEM((ROWS + 2 * H, 128), jnp.float32),
                pltpu.VMEM((9, ROWS, 128), jnp.float32),
                pltpu.SemaphoreType.DMA((7,)),
                pltpu.SemaphoreType.DMA((10,)),
                pltpu.SemaphoreType.DMA((10,)),
            ],
            compiler_params=pltpu.CompilerParams(
                collective_id=0, has_side_effects=True, vmem_limit_bytes=32 * 2**20
            ),
        )(*flat, stiff, buoy, wind.reshape(1, 128))
        return tuple(x.reshape(N, H, 128) for x in out)

    field_spec = P("range", "height", None)
    return jax.shard_map(
        on_device,
        mesh=mesh,
        in_specs=(field_spec,) * 4 + (P("height", None), P("height", None), P()),
        out_specs=(field_spec,) * 4,
        check_vma=False,
    )
```

```python
import jax
import jax.numpy as jnp
from jax import lax
from jax.experimental import pallas as pl
from jax.experimental.pallas import tpu as pltpu
from jax.sharding import PartitionSpec as P

MESH = pl.DeviceIdType.MESH
N = 48
H = 8
HALO = 14
SHIFT = 8
BASE = 3
ROWS = 56
FIRST = 40
UP, DOWN = 7, 6


def planes(ref, start, count):
    rows = pl.ds(pl.multiple_of(start * H, H), count * H)
    return ref[rows, :].reshape(count, H, 128)


def put(ref, start, value):
    rows = pl.ds(pl.multiple_of(start * H, H), value.shape[0] * H)
    ref[rows, :] = value.reshape(value.shape[0] * H, 128)


def row(ref, start, k):
    return ref[pl.ds(start * H + k, H, stride=H), :]


def put_row(ref, start, k, value):
    ref[pl.ds(start * H + k, H, stride=H), :] = value


def lat(value, steps):
    return pltpu.roll(value, steps % 128, 2)


def hgt(value, steps):
    return pltpu.roll(value, steps % H, 1)


def central(x, count):
    return 8.0 * (x[3 : 3 + count] - x[1 : 1 + count]) - (x[4 : 4 + count] - x[0:count])


def flows(src, dst, start, count, to, coef):
    press, vert, radial, lateral = src
    new_vert, new_radial, new_lateral = dst
    p = planes(press, start - 1, count + 3)
    u = planes(radial, start - 2, count + 4)
    v = planes(lateral, start - 2, count + 4)
    w = planes(vert, start - 2, count + 4)
    b1, a1, s0, s1, k0, k1, k2, km = (coef[i] for i in range(8))
    here, mid = p[1 : 1 + count], w[2 : 2 + count]
    put(
        new_radial,
        to,
        u[2 : 2 + count]
        - b1 * (27.0 * (p[2 : 2 + count] - here) - (p[3 : 3 + count] - p[0:count]))
        - a1 * central(u, count)
        - (s0 * mid + s1 * hgt(mid, 1)),
    )
    put(
        new_lateral,
        to,
        v[2 : 2 + count]
        - b1 * (27.0 * (lat(here, -1) - here) - (lat(here, -2) - lat(here, 1)))
        - a1 * central(v, count),
    )
    put(
        new_vert,
        to,
        mid
        + (k0 * here - k1 * hgt(here, -1))
        + (k2 * hgt(here, -2) - km * hgt(here, 1))
        - a1 * central(w, count),
    )


def pressures(press, new, dst, start, at, count, to, coef):
    new_vert, new_radial, new_lateral = new
    p = planes(press, start - 2, count + 4)
    u = planes(new_radial, at - 2, count + 3)
    v = planes(new_lateral, at, count)
    w = planes(new_vert, at, count)
    c1, a1, d1, d2, dm = coef[8], coef[1], coef[9], coef[10], coef[11]
    spread = (
        27.0 * (u[2 : 2 + count] - u[1 : 1 + count])
        - (u[3 : 3 + count] - u[0:count])
        + 27.0 * (v - lat(v, 1))
        - (lat(v, -1) - lat(v, 2))
        + (27.0 * w - d1 * hgt(w, 1))
        - (dm * hgt(w, -1) - d2 * hgt(w, 2))
    )
    put(dst, to, p[2 : 2 + count] - c1 * spread - a1 * central(p, count))


def line(ref, i):
    return jnp.broadcast_to(ref[pl.ds(i, 1), :], (H, 128))


def changes(coef, low_p, high_p, high_p2):
    b24 = coef.at[0]
    return (
        -line(b24, 0) * low_p,
        line(b24, 6) * high_p,
        line(b24, 7) * (high_p2 - 27.0 * high_p),
    )


def correct_pressure(ref, at, coef, du, d0, d6, d7, low1, low2, high):
    c24 = coef.at[8]
    for i, add in (
        (0, du + 27.0 * (d0 - low1) + low2),
        (1, low1 - 27.0 * d0),
        (2, d0),
        (5, -d6),
        (6, 27.0 * d6 - d7),
        (7, 27.0 * (d7 - d6) - high),
    ):
        put_row(ref, at, i, row(ref, at, i) - line(c24, i) * add)


def add_row(ref, at, i, value):
    new = row(ref, at, i) + value
    put_row(ref, at, i, new)
    return new


def first_step(
    ranges,
    heights,
    press_in,
    vert_in,
    radial_in,
    lateral_in,
    stiff_in,
    buoy_in,
    wind_in,
    p1,
    w1,
    u1,
    v1,
    halo,
    coef,
    low_more,
    high_more,
    p0,
    w0,
    u0,
    v0,
    stiff,
    buoy,
    wind,
    up_send,
    up_recv,
    down_send,
    down_recv,
    up_more,
    down_more,
    low_w,
    local_sem,
    send_sem,
    recv_sem,
    ready,
):
    r, h = lax.axis_index("range"), lax.axis_index("height")
    first_r, last_r = r == 0, r == ranges - 1
    first_h, last_h = h == 0, h == heights - 1
    left = (lax.rem(r + ranges - 1, ranges), h)
    right = (lax.rem(r + 1, ranges), h)
    below = (r, lax.rem(h + heights - 1, heights))
    above = (r, lax.rem(h + 1, heights))
    no_left, no_right = jnp.logical_not(first_r), jnp.logical_not(last_r)
    no_below, no_above = jnp.logical_not(first_h), jnp.logical_not(last_h)
    odd = lax.rem(h, 2) == 1
    is_late = lax.rem(h // 2, 2) == 1
    is_early = jnp.logical_not(is_late)
    even = jnp.logical_not(odd)
    far_up, far_down = jnp.logical_and(odd, no_above), jnp.logical_and(even, no_below)
    near_up, near_down = jnp.logical_and(even, no_above), jnp.logical_and(odd, no_below)

    barrier = pltpu.get_barrier_semaphore()
    for there, device in (
        (no_right, right),
        (near_up, above),
        (near_down, below),
        (jnp.logical_and(is_early, far_up), above),
        (jnp.logical_and(is_early, far_down), below),
    ):

        @pl.when(there)
        def _():
            pl.semaphore_signal(barrier, inc=1, device_id=device, device_id_type=MESH)

    whole = pl.ds(0, N * H)
    loads = [
        pltpu.make_async_copy(src, dst, local_sem.at[i])
        for i, (src, dst) in enumerate(
            (
                (buoy_in, buoy),
                (stiff_in, stiff),
                (wind_in, wind),
                (press_in, p0.at[whole]),
                (vert_in, w0.at[whole]),
                (radial_in, u0.at[whole]),
                (lateral_in, v0.at[whole]),
            )
        )
    ]
    for load in loads:
        load.start()
    def remote(src, dst, i, device):
        return pltpu.make_async_remote_copy(
            src_ref=src,
            dst_ref=dst,
            send_sem=send_sem.at[i],
            recv_sem=recv_sem.at[i],
            device_id=device,
            device_id_type=MESH,
        )

    early, late = pl.ds(0, FIRST), pl.ds(FIRST, ROWS - FIRST)
    head, tail = pl.ds(0, HALO * H), pl.ds(N * H, HALO * H)
    ups = [
        remote(up_send.at[:, early], up_recv.at[:, early], 0, above),
        remote(up_send.at[:, late], up_recv.at[:, late], 1, above),
        remote(up_more, low_more, 2, above),
    ]
    downs = [
        remote(down_send.at[:, early], down_recv.at[:, early], 3, below),
        remote(down_send.at[:, late], down_recv.at[:, late], 4, below),
        remote(down_more, high_more, 5, below),
    ]
    lefts = [
        remote(src.at[head], dst.at[tail], 6 + i, left)
        for i, (src, dst) in enumerate(
            ((press_in, p0), (radial_in, u0), (vert_in, w0), (lateral_in, v0))
        )
    ]

    late_far = jnp.logical_and(is_late, jnp.logical_or(far_up, far_down))
    early_far = jnp.logical_and(is_early, jnp.logical_or(far_up, far_down))
    peers = sum(
        there.astype(jnp.int32)
        for there in (no_left, jnp.logical_or(near_up, near_down), late_far)
    )
    pl.semaphore_wait(barrier, peers)

    for there, device in ((far_up, above), (far_down, below)):

        @pl.when(jnp.logical_and(is_late, there))
        def _():
            pl.semaphore_signal(ready, inc=1, device_id=device, device_id_type=MESH)

    @pl.when(no_left)
    def _():
        for copy in lefts:
            copy.start()

    for load in loads[:3]:
        load.wait()

    k = lax.broadcasted_iota(jnp.int32, (H, 128), 0)
    lane = lax.broadcasted_iota(jnp.int32, (H, 128), 1)
    spread_wind = jnp.broadcast_to(wind[...], (H, 128))
    top = heights * H - 1

    def wind_at(rows):
        chosen = jnp.where(lane == rows, spread_wind, 0.0)
        return jnp.broadcast_to(jnp.sum(chosen, axis=1, keepdims=True), (H, 128))

    def shear_at(rows):
        upper = wind_at(jnp.where(rows < top, rows + 1, top))
        lower = wind_at(jnp.where(rows > 0, rows - 1, 0))
        return 0.5 * (upper - lower)

    mine = k + h * H
    b24, c24 = buoy[...] * (1.0 / 24.0), stiff[...] * (1.0 / 24.0)
    a12 = wind_at(mine) * (1.0 / 12.0)
    half_shear = 0.5 * shear_at(mine)
    b27 = b24 * 27.0
    full = jnp.full((H, 128), 27.0, jnp.float32)
    one = jnp.full((H, 128), 1.0, jnp.float32)
    for i, value in enumerate(
        (
            b24,
            a12,
            half_shear,
            jnp.where(k > 0, half_shear, 0.0),
            b27,
            jnp.where(k < H - 1, b27, 0.0),
            jnp.where(k < H - 2, b24, 0.0),
            jnp.where(k > 0, b24, 0.0),
            c24,
            jnp.where(k > 0, full, 0.0),
            jnp.where(k > 1, one, 0.0),
            jnp.where(k < H - 1, one, 0.0),
        )
    ):
        coef[i] = value
    for i, outside in enumerate((-1, -2, H)):
        coef[12 + i] = wind_at(jnp.zeros_like(k) + (h * H + outside)) * (1.0 / 12.0)
    s_low = 0.5 * shear_at(jnp.zeros_like(k) + h * H)
    s_high = 0.5 * shear_at(jnp.zeros_like(k) + (h * H + H))
    coef[15] = s_low

    up_more[pl.ds(0, H), :] = b24
    down_more[pl.ds(0, H), :] = b24
    up_more[pl.ds(H, H), :] = c24
    down_more[pl.ds(H, H), :] = c24

    def free_flows(start, step, times):
        def body(j, carry):
            at = start + step * j
            flows((p0, w0, u0, v0), (w1, u1, v1), at, step, at, coef)
            return carry

        lax.fori_loop(0, times, body, 0)

    def free_pressures(start, step, times):
        def body(j, carry):
            at = start + step * j
            pressures(p0, (w1, u1, v1), p1, at, at, step, at, coef)
            return carry

        lax.fori_loop(0, times, body, 0)

    def pack(first, last):
        def body(j, carry):
            at = BASE + H * j
            to = pl.ds(pl.multiple_of(j * H, H), H)
            for q, (ref, height) in enumerate(
                ((p0, 7), (w0, 7), (w1, 7), (w1, 6), (p1, 7), (p1, 6), (p1, 5))
            ):
                up_send[q, to, :] = row(ref, at, height)
            for q, (ref, height) in enumerate(
                ((p0, 0), (p0, 1), (w1, 0), (p1, 0), (p1, 1), (p1, 2))
            ):
                down_send[q, to, :] = row(ref, at, height)
            return carry

        lax.fori_loop(first, last, body, 0)

    for load in loads[3:]:
        load.wait()
    free_flows(BASE, 6, 7)
    free_pressures(BASE, 5, 8)
    pack(0, FIRST // H)

    def send(i):
        for there, copies in ((far_up, ups), (far_down, downs)):
            pl.when(jnp.logical_and(is_late, there))(copies[i].start)
        for there, copies in ((near_up, ups), (near_down, downs)):
            pl.when(there)(copies[i].start)

    send(0)

    nothing = jnp.zeros((HALO * H, 128), jnp.float32)

    @pl.when(last_r)
    def _():
        for ref in (p0, u0, w0, v0):
            ref[tail, :] = nothing

    @pl.when(no_right)
    def _():
        for copy in lefts:
            copy.wait_recv()

    free_flows(45, 5, 3)

    def clear_after():
        for ref in (u1, v1, w1, p1):
            ref[pl.ds(N * H, 12 * H), :] = jnp.zeros((12 * H, 128), jnp.float32)

    pl.when(last_r)(clear_after)
    free_pressures(43, 4, 4)
    pl.when(last_r)(clear_after)
    pack(FIRST // H, ROWS // H)
    last = row(w0, BASE + ROWS - H + 1, 7)
    up_more[pl.ds(2 * H, H), :] = last

    send(1)
    send(2)

    @pl.when(early_far)
    def _():
        pl.semaphore_wait(ready, 1)

    for there, copies in ((far_up, ups), (far_down, downs)):

        @pl.when(jnp.logical_and(is_early, there))
        def _():
            for copy in copies:
                copy.start()

    @pl.when(no_below)
    def _():
        for copy in ups:
            copy.wait_recv()

    @pl.when(no_above)
    def _():
        for copy in downs:
            copy.wait_recv()

    @pl.when(first_h)
    def _():
        up_recv[...] = jnp.zeros(up_recv.shape, jnp.float32)
        low_more[...] = jnp.zeros(low_more.shape, jnp.float32)

    @pl.when(last_h)
    def _():
        down_recv[...] = jnp.zeros(down_recv.shape, jnp.float32)
        high_more[...] = jnp.zeros(high_more.shape, jnp.float32)

    low_w[pl.ds(0, H), :] = jnp.zeros((H, 128), jnp.float32)
    low_w[pl.ds(H, ROWS), :] = up_recv[1]
    low_w[pl.ds(H + ROWS, H), :] = jnp.broadcast_to(
        low_more[pl.ds(3 * H - 1, 1), :], (H, 128)
    )
    first_plane = jnp.where(first_r, SHIFT, 0)
    after_plane = jnp.where(last_r, N, 2 * N)

    def correct_first(j, carry):
        at = BASE + H * j
        here = pl.ds(pl.multiple_of(j * H, H), H)
        low_p0, low_w1, low_w2 = up_recv[0, here, :], up_recv[2, here, :], up_recv[3, here, :]
        high_p0, high_p0b = down_recv[0, here, :], down_recv[1, here, :]
        wl = [low_w[pl.ds(j * H + H + s, H), :] for s in (-2, -1, 0, 1)]
        wt = [row(w0, at + s, 7) for s in (-2, -1, 0, 1)]
        own_p0, own_p1, own_p7 = row(p0, at, 0), row(p0, at, 1), row(p0, at, 7)
        e1 = line(low_more, 7) * (own_p1 - 27.0 * own_p0)
        e2 = line(low_more, 6) * own_p0
        e8 = line(high_more, 0) * own_p7 * -1.0
        low_w1, low_w2 = low_w1 + e1, low_w2 + e2
        high_w = down_recv[2, here, :] + e8
        d0, d6, d7 = changes(coef, low_p0, high_p0, high_p0b)
        new0, new6, new7 = (add_row(w1, at, i, d) for i, d in ((0, d0), (6, d6), (7, d7)))
        add_row(u1, at, 0, -s_low * wl[2])
        du = -s_low * (27.0 * (wl[2] - wl[1]) - (wl[3] - wl[0]))
        correct_pressure(p1, at, coef, du, d0, d6, d7, low_w1, low_w2, high_w)
        du_high = -s_high * (27.0 * (wt[2] - wt[1]) - (wt[3] - wt[0]))
        low_p1 = up_recv[4, here, :] - line(low_more, H + 7) * (27.0 * (e1 - e2) - new0)
        low_p2 = up_recv[5, here, :] - line(low_more, H + 6) * (27.0 * e2 - e1)
        low_p3 = up_recv[6, here, :] + line(low_more, H + 5) * e2
        high_p1 = down_recv[3, here, :] - line(high_more, H) * (
            du_high + 27.0 * (e8 - new7) + new6
        )
        high_p2 = down_recv[4, here, :] - line(high_more, H + 1) * (new7 - 27.0 * e8)
        high_p3 = down_recv[5, here, :] - line(high_more, H + 2) * e8
        plane = k + at
        keep = jnp.logical_and(plane >= first_plane, plane < after_plane)
        for i, value in enumerate(
            (low_w1, low_w2, low_p1, low_p2, low_p3, high_w, high_p1, high_p2, high_p3)
        ):
            halo[i, here, :] = jnp.where(keep, value, 0.0)
        return carry

    lax.fori_loop(0, ROWS // H, correct_first, 0)

    @pl.when(first_r)
    def _():
        for ref in (u1, v1, w1, p1):
            ref[pl.ds(0, SHIFT * H), :] = jnp.zeros((SHIFT * H, 128), jnp.float32)

    pl.when(last_r)(clear_after)

    @pl.when(no_above)
    def _():
        for copy in ups:
            copy.wait_send()

    @pl.when(no_below)
    def _():
        for copy in downs:
            copy.wait_send()

    @pl.when(no_left)
    def _():
        for copy in lefts:
            copy.wait_send()


def second_step(
    p1,
    w1,
    u1,
    v1,
    halo,
    coef,
    low_more,
    high_more,
    press_out,
    vert_out,
    radial_out,
    lateral_out,
    p2,
    w2,
    u2,
    v2,
    sems,
):
    first_r = lax.axis_index("range") == 0
    def second_flows(j, carry):
        at = 8 * j
        flows((p1, w1, u1, v1), (w2, u2, v2), at + SHIFT, 8, at + 2, coef)
        return carry

    lax.fori_loop(0, N // 8, second_flows, 0)
    flows((p1, w1, u1, v1), (w2, u2, v2), SHIFT - 2, 2, 0, coef)
    flows((p1, w1, u1, v1), (w2, u2, v2), SHIFT + N, 1, N + 2, coef)

    @pl.when(first_r)
    def _():
        u2[pl.ds(0, 2 * H), :] = jnp.zeros((2 * H, 128), jnp.float32)

    def second_pressures(j, carry):
        at = 8 * j
        pressures(p1, (w2, u2, v2), p2, at + SHIFT, at + 2, 8, at, coef)
        return carry

    lax.fori_loop(0, N // 8, second_pressures, 0)

    def correct_second(j, carry):
        at = H * j
        off = at + SHIFT - BASE

        def rows_of(i, s=0):
            return halo[i, pl.ds(off + s, H), :]

        def across(i):
            return 8.0 * (rows_of(i, 1) - rows_of(i, -1)) - (rows_of(i, 2) - rows_of(i, -2))

        low_w1, low_w2, low_p1, low_p2, low_p3, high_w, high_p1, high_p2, high_p3 = (
            rows_of(i) for i in range(9)
        )
        own_p0, own_p1, own_p7 = (row(p1, at + SHIFT, i) for i in (0, 1, 7))
        d0, d6, d7 = changes(coef, low_p1, high_p1, high_p2)
        for i, d in ((0, d0), (6, d6), (7, d7)):
            add_row(w2, at + 2, i, d)
        add_row(u2, at + 2, 0, -coef[15] * low_w1)
        du = -coef[15] * (
            27.0 * (low_w1 - rows_of(0, -1)) - (rows_of(0, 1) - rows_of(0, -2))
        )
        new1 = (
            low_w1
            - line(low_more, 7) * (27.0 * (own_p0 - low_p1) - (own_p1 - low_p2))
            - coef[12] * across(0)
        )
        new2 = (
            low_w2
            - line(low_more, 6) * (27.0 * (low_p1 - low_p2) - (own_p0 - low_p3))
            - coef[13] * across(1)
        )
        new8 = (
            high_w
            - line(high_more, 0) * (27.0 * (high_p2 - high_p1) - (high_p3 - own_p7))
            - coef[14] * across(5)
        )
        correct_pressure(p2, at, coef, du, d0, d6, d7, new1, new2, new8)
        return carry

    lax.fori_loop(0, N // H, correct_second, 0)

    inner = pl.ds(2 * H, N * H)
    stores = [
        pltpu.make_async_copy(src, dst, sems.at[i])
        for i, (src, dst) in enumerate(
            (
                (p2, press_out),
                (w2.at[inner], vert_out),
                (u2.at[inner], radial_out),
                (v2.at[inner], lateral_out),
            )
        )
    ]
    for store in stores:
        store.start()

    for store in stores:
        store.wait()


def solution(mesh):
    ranges, heights = mesh.shape["range"], mesh.shape["height"]

    def on_device(press, vert, radial, lateral, stiff, buoy, wind):
        def field(count):
            return pltpu.VMEM((count * H, 128), jnp.float32)

        flat = [x.reshape(N * H, 128) for x in (press, vert, radial, lateral)]
        arguments = [
            pltpu.with_memory_space_constraint(x, pltpu.HBM)
            for x in (*flat, stiff, buoy, wind.reshape(1, 128))
        ]
        state = pl.pallas_call(
            lambda *refs: first_step(ranges, heights, *refs),
            out_shape=[field(64)] * 4
            + [
                pltpu.VMEM((9, ROWS, 128), jnp.float32),
                pltpu.VMEM((16, H, 128), jnp.float32),
                field(3),
                field(2),
            ],
            in_specs=[pl.BlockSpec(memory_space=pltpu.HBM)] * 7,
            out_specs=[pl.BlockSpec(memory_space=pltpu.VMEM)] * 8,
            scratch_shapes=[field(64)] * 4
            + [
                field(1),
                field(1),
                pltpu.VMEM((1, 128), jnp.float32),
                pltpu.VMEM((UP, ROWS, 128), jnp.float32),
                pltpu.VMEM((UP, ROWS, 128), jnp.float32),
                pltpu.VMEM((DOWN, ROWS, 128), jnp.float32),
                pltpu.VMEM((DOWN, ROWS, 128), jnp.float32),
                field(3),
                field(2),
                pltpu.VMEM((ROWS + 2 * H, 128), jnp.float32),
                pltpu.SemaphoreType.DMA((7,)),
                pltpu.SemaphoreType.DMA((10,)),
                pltpu.SemaphoreType.DMA((10,)),
                pltpu.SemaphoreType.REGULAR,
            ],
            compiler_params=pltpu.CompilerParams(
                collective_id=0, has_side_effects=True, vmem_limit_bytes=24 * 2**20
            ),
        )(*arguments)
        out = pl.pallas_call(
            second_step,
            out_shape=[jax.ShapeDtypeStruct((N * H, 128), jnp.float32)] * 4,
            in_specs=[pl.BlockSpec(memory_space=pltpu.VMEM)] * 8,
            out_specs=[pl.BlockSpec(memory_space=pltpu.HBM)] * 4,
            scratch_shapes=[field(N), field(N + 4), field(N + 4), field(N + 4)]
            + [pltpu.SemaphoreType.DMA((4,))],
            compiler_params=pltpu.CompilerParams(vmem_limit_bytes=24 * 2**20),
        )(*state)
        return tuple(x.reshape(N, H, 128) for x in out)

    field_spec = P("range", "height", None)
    return jax.shard_map(
        on_device,
        mesh=mesh,
        in_specs=(field_spec,) * 4 + (P("height", None), P("height", None), P()),
        out_specs=(field_spec,) * 4,
        check_vma=False,
    )
```

```python
import functools

import jax
import jax.numpy as jnp
from jax import lax
from jax.experimental import pallas as pl
from jax.experimental.pallas import tpu as pltpu
from jax.sharding import PartitionSpec as P

MESH = pl.DeviceIdType.MESH
N = 48
H = 8
HALO = 14
SHIFT = 8
BASE = 3
ROWS = 56
FIRST = 40
REST = ROWS - FIRST
PART = 32
UP, DOWN = 7, 6
LINE = 8


def planes(ref, start, count):
    rows = pl.ds(pl.multiple_of(start * H, H), count * H)
    return ref[rows, :].reshape(count, H, 128)


def put(ref, start, value):
    rows = pl.ds(pl.multiple_of(start * H, H), value.shape[0] * H)
    ref[rows, :] = value.reshape(value.shape[0] * H, 128)


def row(ref, start, k):
    return ref[pl.ds(start * H + k, H, stride=H), :]


def put_row(ref, start, k, value):
    ref[pl.ds(start * H + k, H, stride=H), :] = value


def lat(value, steps):
    return pltpu.roll(value, steps % 128, 2)


def hgt(value, steps):
    return pltpu.roll(value, steps % H, 1)


def central(x, count):
    return 8.0 * (x[3 : 3 + count] - x[1 : 1 + count]) - (x[4 : 4 + count] - x[0:count])


def flows(src, dst, start, count, to, coef):
    press, vert, radial, lateral = src
    new_vert, new_radial, new_lateral = dst
    p = planes(press, start - 1, count + 3)
    u = planes(radial, start - 2, count + 4)
    v = planes(lateral, start - 2, count + 4)
    w = planes(vert, start - 2, count + 4)
    b1, a1, s0, s1, k0, k1, k2, km = (coef[i] for i in range(8))
    here, mid = p[1 : 1 + count], w[2 : 2 + count]
    put(
        new_radial,
        to,
        u[2 : 2 + count]
        - b1 * (27.0 * (p[2 : 2 + count] - here) - (p[3 : 3 + count] - p[0:count]))
        - a1 * central(u, count)
        - (s0 * mid + s1 * hgt(mid, 1)),
    )
    put(
        new_lateral,
        to,
        v[2 : 2 + count]
        - b1 * (27.0 * (lat(here, -1) - here) - (lat(here, -2) - lat(here, 1)))
        - a1 * central(v, count),
    )
    put(
        new_vert,
        to,
        mid
        + (k0 * here - k1 * hgt(here, -1))
        + (k2 * hgt(here, -2) - km * hgt(here, 1))
        - a1 * central(w, count),
    )


def pressures(press, new, dst, start, at, count, to, coef):
    new_vert, new_radial, new_lateral = new
    p = planes(press, start - 2, count + 4)
    u = planes(new_radial, at - 2, count + 3)
    v = planes(new_lateral, at, count)
    w = planes(new_vert, at, count)
    c1, a1, d1, d2, dm = coef[8], coef[1], coef[9], coef[10], coef[11]
    spread = (
        27.0 * (u[2 : 2 + count] - u[1 : 1 + count])
        - (u[3 : 3 + count] - u[0:count])
        + 27.0 * (v - lat(v, 1))
        - (lat(v, -1) - lat(v, 2))
        + (27.0 * w - d1 * hgt(w, 1))
        - (dm * hgt(w, -1) - d2 * hgt(w, 2))
    )
    put(dst, to, p[2 : 2 + count] - c1 * spread - a1 * central(p, count))


def line(ref, i):
    return jnp.broadcast_to(ref[pl.ds(i, 1), :], (H, 128))


def changes(coef, low_p, high_p, high_p2):
    b24 = coef.at[0]
    return (
        -line(b24, 0) * low_p,
        line(b24, 6) * high_p,
        line(b24, 7) * (high_p2 - 27.0 * high_p),
    )


def correct_pressure(ref, at, coef, du, d0, d6, d7, low1, low2, high):
    c24 = coef.at[8]
    for i, add in (
        (0, du + 27.0 * (d0 - low1) + low2),
        (1, low1 - 27.0 * d0),
        (2, d0),
        (5, -d6),
        (6, 27.0 * d6 - d7),
        (7, 27.0 * (d7 - d6) - high),
    ):
        put_row(ref, at, i, row(ref, at, i) - line(c24, i) * add)


def add_row(ref, at, i, value):
    new = row(ref, at, i) + value
    put_row(ref, at, i, new)
    return new


def both_steps(
    ranges,
    heights,
    press_in,
    vert_in,
    radial_in,
    lateral_in,
    stiff_in,
    buoy_in,
    wind_in,
    p2,
    w2,
    u2,
    v2,
    p0,
    w0,
    u0,
    v0,
    p1,
    w1,
    u1,
    v1,
    stiff,
    buoy,
    wind,
    up_send,
    up_recv,
    down_send,
    down_recv,
    low_w,
    halo,
    coef,
    low_more,
    high_more,
    local_sem,
    send_sem,
    recv_sem,
    ready,
):
    r, h = lax.axis_index("range"), lax.axis_index("height")
    first_r, last_r = r == 0, r == ranges - 1
    first_h, last_h = h == 0, h == heights - 1
    left = (lax.rem(r + ranges - 1, ranges), h)
    right = (lax.rem(r + 1, ranges), h)
    below = (r, lax.rem(h + heights - 1, heights))
    above = (r, lax.rem(h + 1, heights))
    no_left, no_right = jnp.logical_not(first_r), jnp.logical_not(last_r)
    no_below, no_above = jnp.logical_not(first_h), jnp.logical_not(last_h)
    odd = lax.rem(h, 2) == 1
    is_late = lax.rem(h // 2, 2) == 1
    is_early = jnp.logical_not(is_late)
    even = jnp.logical_not(odd)
    far_up, far_down = jnp.logical_and(odd, no_above), jnp.logical_and(even, no_below)
    near_up, near_down = jnp.logical_and(even, no_above), jnp.logical_and(odd, no_below)

    barrier = pltpu.get_barrier_semaphore()
    for there, device in (
        (no_right, right),
        (near_up, above),
        (near_down, below),
        (jnp.logical_and(is_early, far_up), above),
        (jnp.logical_and(is_early, far_down), below),
    ):

        @pl.when(there)
        def _():
            pl.semaphore_signal(barrier, inc=1, device_id=device, device_id_type=MESH)

    whole = pl.ds(0, N * H)
    loads = [
        pltpu.make_async_copy(src, dst, local_sem.at[i])
        for i, (src, dst) in enumerate(
            (
                (buoy_in, buoy),
                (stiff_in, stiff),
                (wind_in, wind),
                (press_in, p0.at[whole]),
                (vert_in, w0.at[whole]),
                (radial_in, u0.at[whole]),
                (lateral_in, v0.at[whole]),
            )
        )
    ]
    for load in loads:
        load.start()
    def remote(src, dst, i, device):
        return pltpu.make_async_remote_copy(
            src_ref=src,
            dst_ref=dst,
            send_sem=send_sem.at[i],
            recv_sem=recv_sem.at[i],
            device_id=device,
            device_id_type=MESH,
        )

    head, tail = pl.ds(0, HALO * H), pl.ds(N * H, HALO * H)
    ups = [remote(up_send[i], up_recv[i], i, above) for i in range(3)]
    downs = [remote(down_send[i], down_recv[i], 3 + i, below) for i in range(3)]
    lefts = [
        remote(src.at[head], dst.at[tail], 6 + i, left)
        for i, (src, dst) in enumerate(
            ((press_in, p0), (radial_in, u0), (vert_in, w0), (lateral_in, v0))
        )
    ]

    late_far = jnp.logical_and(is_late, jnp.logical_or(far_up, far_down))
    early_far = jnp.logical_and(is_early, jnp.logical_or(far_up, far_down))
    peers = sum(
        there.astype(jnp.int32)
        for there in (no_left, jnp.logical_or(near_up, near_down), late_far)
    )
    place = lax.rem(r, LINE)
    waits_long = jnp.logical_and(is_early, place == 0)

    def greet():
        pl.semaphore_wait(barrier, peers)
        for there, device in ((far_up, above), (far_down, below)):

            @pl.when(jnp.logical_and(is_late, there))
            def _():
                pl.semaphore_signal(ready, inc=1, device_id=device, device_id_type=MESH)

        @pl.when(no_left)
        def _():
            for copy in lefts:
                copy.start()

    pl.when(jnp.logical_not(waits_long))(greet)

    for load in loads[:3]:
        load.wait()

    k = lax.broadcasted_iota(jnp.int32, (H, 128), 0)
    lane = lax.broadcasted_iota(jnp.int32, (H, 128), 1)
    spread_wind = jnp.broadcast_to(wind[...], (H, 128))
    top = heights * H - 1

    def wind_at(rows):
        chosen = jnp.where(lane == rows, spread_wind, 0.0)
        return jnp.broadcast_to(jnp.sum(chosen, axis=1, keepdims=True), (H, 128))

    def shear_at(rows):
        upper = wind_at(jnp.where(rows < top, rows + 1, top))
        lower = wind_at(jnp.where(rows > 0, rows - 1, 0))
        return 0.5 * (upper - lower)

    mine = k + h * H
    b24, c24 = buoy[...] * (1.0 / 24.0), stiff[...] * (1.0 / 24.0)
    a12 = wind_at(mine) * (1.0 / 12.0)
    half_shear = 0.5 * shear_at(mine)
    b27 = b24 * 27.0
    full = jnp.full((H, 128), 27.0, jnp.float32)
    one = jnp.full((H, 128), 1.0, jnp.float32)
    for i, value in enumerate(
        (
            b24,
            a12,
            half_shear,
            jnp.where(k > 0, half_shear, 0.0),
            b27,
            jnp.where(k < H - 1, b27, 0.0),
            jnp.where(k < H - 2, b24, 0.0),
            jnp.where(k > 0, b24, 0.0),
            c24,
            jnp.where(k > 0, full, 0.0),
            jnp.where(k > 1, one, 0.0),
            jnp.where(k < H - 1, one, 0.0),
        )
    ):
        coef[i] = value
    for i, outside in enumerate((-1, -2, H)):
        coef[12 + i] = wind_at(jnp.zeros_like(k) + (h * H + outside)) * (1.0 / 12.0)
    s_low = 0.5 * shear_at(jnp.zeros_like(k) + h * H)
    s_high = 0.5 * shear_at(jnp.zeros_like(k) + (h * H + H))

    def free_flows(start, step, times):
        def body(j, carry):
            at = start + step * j
            flows((p0, w0, u0, v0), (w1, u1, v1), at, step, at, coef)
            return carry

        lax.fori_loop(0, times, body, 0)

    def free_pressures(start, step, times):
        def body(j, carry):
            at = start + step * j
            pressures(p0, (w1, u1, v1), p1, at, at, step, at, coef)
            return carry

        lax.fori_loop(0, times, body, 0)

    up_rows = ((p0, 7), (w0, 7)), ((w1, 7), (w1, 6)), ((p1, 7), (p1, 6), (p1, 5))
    down_rows = ((p0, 0), (p0, 1)), ((w1, 0),), ((p1, 0), (p1, 1), (p1, 2))

    def pack(buffer, to, rows, start, count):
        def body(j, carry):
            for q, (ref, height) in enumerate(rows):
                at = pl.ds(pl.multiple_of(to + q * count + j * H, H), H)
                buffer[at, :] = row(ref, start + H * j, height)
            return carry

        lax.fori_loop(0, count // H, body, 0)

    sides = (up_send, up_rows), (down_send, down_rows)

    def send(i):
        for there, copies in ((far_up, ups), (far_down, downs)):
            pl.when(jnp.logical_and(is_late, there))(copies[i].start)
        for there, copies in ((near_up, ups), (near_down, downs)):
            pl.when(there)(copies[i].start)

    for load in loads[3:]:
        load.wait()
    for buffers, (given, _, _) in sides:
        pack(buffers[0], 0, given, BASE, FIRST)
    next_w = line(w0, (BASE + FIRST) * H + 7)
    for_above = jnp.where(k == 3, next_w, jnp.where(k > 3, c24, pltpu.roll(b24, 2, 0)))
    up_send[0][pl.ds(2 * FIRST, H), :] = for_above
    down_send[0][pl.ds(2 * FIRST, H), :] = jnp.where(k < 4, c24, pltpu.roll(b24, 7, 0))
    pl.when(jnp.logical_not(waits_long))(lambda: send(0))
    free_flows(BASE, 6, 7)
    free_pressures(BASE, 5, 8)
    for buffers, (_, flow_rows, press_rows) in sides:
        pack(buffers[1], 0, flow_rows, BASE, FIRST)
        pack(buffers[1], len(flow_rows) * FIRST, press_rows, SHIFT, PART)

    @pl.when(waits_long)
    def _():
        greet()
        send(0)

    send(1)

    nothing = jnp.zeros((HALO * H, 128), jnp.float32)

    @pl.when(last_r)
    def _():
        for ref in (p0, u0, w0, v0):
            ref[tail, :] = nothing

    @pl.when(no_right)
    def _():
        for copy in lefts:
            copy.wait_recv()

    free_flows(45, 5, 3)

    def clear_after():
        for ref in (u1, v1, w1, p1):
            ref[pl.ds(N * H, 12 * H), :] = jnp.zeros((12 * H, 128), jnp.float32)

    pl.when(last_r)(clear_after)
    free_pressures(43, 4, 4)
    pl.when(last_r)(clear_after)
    for buffers, (given, flow_rows, press_rows) in sides:
        pack(buffers[2], 0, given + flow_rows, BASE + FIRST, REST)
        pack(buffers[2], len(given + flow_rows) * REST, press_rows, SHIFT + PART, REST)
    up_send[2][pl.ds(UP * REST, H), :] = row(w0, BASE + ROWS - H + 1, 7)
    send(2)

    for there, outgoing in ((far_up, ups), (far_down, downs)):

        @pl.when(jnp.logical_and(there, is_early))
        def _():
            pl.semaphore_wait(ready, 1)
            for copy in outgoing:
                copy.start()

    first_plane = jnp.where(first_r, SHIFT, 0)
    after_plane = jnp.where(last_r, N, 2 * N)

    def zero(ref, start, count):
        ref[pl.ds(start, count), :] = jnp.zeros((count, 128), jnp.float32)

    def arrived(parts):
        for none, some, copies, buffers in (
            (first_h, no_below, ups, up_recv),
            (last_h, no_above, downs, down_recv),
        ):

            @pl.when(some)
            def _():
                for i in parts:
                    copies[i].wait_recv()

            @pl.when(none)
            def _():
                for i in parts:
                    zero(buffers[i], 0, buffers[i].shape[0])

    def tile(ref, at):
        return ref[pl.ds(pl.multiple_of(at, H), H), :]

    def first_part(buffers, q, j):
        ref, at = (buffers[0], q) if q < 2 else (buffers[1], q - 2)
        return tile(ref, at * FIRST + j * H)

    def last_part(buffers, q, j):
        return tile(buffers[2], q * REST - FIRST + j * H)

    def first_pressure(buffers, flow_rows, q, j):
        return tile(buffers[1], flow_rows * FIRST + q * PART + j * H)

    def last_pressure(buffers, flow_rows, q, j):
        return tile(buffers[2], (2 + flow_rows + q) * REST - PART + j * H)

    def own_parts(at):
        own_p0, own_p1, own_p7 = row(p0, at, 0), row(p0, at, 1), row(p0, at, 7)
        return (
            line(low_more, 1) * (own_p1 - 27.0 * own_p0),
            line(low_more, 0) * own_p0,
            -line(high_more, 7) * own_p7,
        )

    def correct_first(part, j, carry):
        at = BASE + H * j
        here = pl.ds(pl.multiple_of(j * H, H), H)
        low_p0, _, low_w1, low_w2 = (part(up_recv, q, j) for q in range(4))
        high_p0, high_p1, high_w = (part(down_recv, q, j) for q in range(3))
        wl = [low_w[pl.ds(j * H + H + s, H), :] for s in (-2, -1, 0, 1)]
        e1, e2, e8 = own_parts(at)
        low_w1, low_w2, high_w = low_w1 + e1, low_w2 + e2, high_w + e8
        d0, d6, d7 = changes(coef, low_p0, high_p0, high_p1)
        for i, d in ((0, d0), (6, d6), (7, d7)):
            add_row(w1, at, i, d)
        add_row(u1, at, 0, -s_low * wl[2])
        du = -s_low * (27.0 * (wl[2] - wl[1]) - (wl[3] - wl[0]))
        correct_pressure(p1, at, coef, du, d0, d6, d7, low_w1, low_w2, high_w)
        plane = k + at
        keep = jnp.logical_and(plane >= first_plane, plane < after_plane)
        for i, value in enumerate((low_w1, low_w2, high_w)):
            halo[i, here, :] = jnp.where(keep, value, 0.0)
        return carry

    def second_flows(start, step, times):
        def body(j, carry):
            at = start + step * j
            flows((p1, w1, u1, v1), (w2, u2, v2), at + SHIFT, step, at + 2, coef)
            return carry

        lax.fori_loop(0, times, body, 0)

    def second_pressures(start, step, times):
        def body(j, carry):
            at = start + step * j
            pressures(p1, (w2, u2, v2), p2, at + SHIFT, at + 2, step, at, coef)
            return carry

        lax.fori_loop(0, times, body, 0)

    def correct_second(part, j, carry):
        at = H * j
        plane = at + SHIFT
        off = plane - BASE

        def rows_of(i, s=0):
            return halo[i, pl.ds(off + s, H), :]

        def across(i):
            return 8.0 * (rows_of(i, 1) - rows_of(i, -1)) - (rows_of(i, 2) - rows_of(i, -2))

        low_w1, low_w2, high_w = (rows_of(i) for i in range(3))
        e1, e2, e8 = own_parts(plane)
        new0, new6, new7 = (row(w1, plane, i) for i in (0, 6, 7))
        wt = [row(w0, plane + s, 7) for s in (-2, -1, 0, 1)]
        du_high = -s_high * (27.0 * (wt[2] - wt[1]) - (wt[3] - wt[0]))
        inside = k + plane < after_plane
        low_p1, low_p2, low_p3, high_p1, high_p2, high_p3 = (
            jnp.where(inside, value, 0.0)
            for value in (
                part(up_recv, 2, 0, j) - line(low_more, 7) * (27.0 * (e1 - e2) - new0),
                part(up_recv, 2, 1, j) - line(low_more, 6) * (27.0 * e2 - e1),
                part(up_recv, 2, 2, j) + line(low_more, 5) * e2,
                part(down_recv, 1, 0, j)
                - line(high_more, 0) * (du_high + 27.0 * (e8 - new7) + new6),
                part(down_recv, 1, 1, j) - line(high_more, 1) * (new7 - 27.0 * e8),
                part(down_recv, 1, 2, j) - line(high_more, 2) * e8,
            )
        )
        own_p0, own_p1, own_p7 = (row(p1, plane, i) for i in (0, 1, 7))
        d0, d6, d7 = changes(coef, low_p1, high_p1, high_p2)
        for i, d in ((0, d0), (6, d6), (7, d7)):
            add_row(w2, at + 2, i, d)
        du = -s_low * (27.0 * (low_w1 - rows_of(0, -1)) - (rows_of(0, 1) - rows_of(0, -2)))
        new1 = (
            low_w1
            - line(low_more, 1) * (27.0 * (own_p0 - low_p1) - (own_p1 - low_p2))
            - coef[12] * across(0)
        )
        new2 = (
            low_w2
            - line(low_more, 0) * (27.0 * (low_p1 - low_p2) - (own_p0 - low_p3))
            - coef[13] * across(1)
        )
        new8 = (
            high_w
            - line(high_more, 7) * (27.0 * (high_p2 - high_p1) - (high_p3 - own_p7))
            - coef[14] * across(2)
        )
        correct_pressure(p2, at, coef, du, d0, d6, d7, new1, new2, new8)
        return carry

    arrived((0, 1))
    more = pl.ds(2 * FIRST, H)
    low_more[...], high_more[...] = up_recv[0][more, :], down_recv[0][more, :]
    zero(low_w, 0, H)
    low_w[pl.ds(H, FIRST), :] = up_recv[0][pl.ds(FIRST, FIRST), :]
    low_w[pl.ds(H + FIRST, H), :] = line(low_more, 3)
    lax.fori_loop(0, FIRST // H, functools.partial(correct_first, first_part), 0)

    @pl.when(first_r)
    def _():
        for ref in (u1, v1, w1, p1):
            zero(ref, 0, SHIFT * H)

    second_flows(-2, 5, 7)
    pl.when(first_r)(lambda: zero(u2, 0, 2 * H))
    second_pressures(0, 8, PART // 8)
    lax.fori_loop(0, PART // H, functools.partial(correct_second, first_pressure), 0)

    arrived((2,))
    low_w[pl.ds(H + FIRST, REST), :] = up_recv[2][pl.ds(REST, REST), :]
    low_w[pl.ds(H + ROWS, H), :] = line(up_recv[2], UP * REST + H - 1)
    lax.fori_loop(FIRST // H, ROWS // H, functools.partial(correct_first, last_part), 0)
    pl.when(last_r)(clear_after)
    second_flows(PART + 1, 8, 2)
    second_pressures(PART, 8, (N - PART) // 8)
    lax.fori_loop(PART // H, N // H, functools.partial(correct_second, last_pressure), 0)

    def correct_radial(j, carry):
        rows = halo[0, pl.ds(H * j + SHIFT - BASE, H), :]
        add_row(u2, H * j + 2, 0, -s_low * rows)
        return carry

    lax.fori_loop(0, N // H, correct_radial, 0)

    @pl.when(no_above)
    def _():
        for copy in ups:
            copy.wait_send()

    @pl.when(no_below)
    def _():
        for copy in downs:
            copy.wait_send()

    @pl.when(no_left)
    def _():
        for copy in lefts:
            copy.wait_send()


def store(p2, w2, u2, v2, press_out, vert_out, radial_out, lateral_out, sems):
    inner = pl.ds(2 * H, N * H)
    copies = [
        pltpu.make_async_copy(src, dst, sems.at[i])
        for i, (src, dst) in enumerate(
            (
                (p2, press_out),
                (w2.at[inner], vert_out),
                (u2.at[inner], radial_out),
                (v2.at[inner], lateral_out),
            )
        )
    ]
    for copy in copies:
        copy.start()
    for copy in copies:
        copy.wait()


def solution(mesh):
    ranges, heights = mesh.shape["range"], mesh.shape["height"]

    def on_device(press, vert, radial, lateral, stiff, buoy, wind):
        def field(count):
            return pltpu.VMEM((count * H, 128), jnp.float32)

        def messages(rows, press_rows, more):
            flow_rows = rows - 2 - press_rows
            first = 2 * FIRST + H
            second = flow_rows * FIRST + press_rows * PART
            third = rows * REST + more * H
            return [pltpu.VMEM((count, 128), jnp.float32) for count in (first, second, third)]

        flat = [x.reshape(N * H, 128) for x in (press, vert, radial, lateral)]
        arguments = [
            pltpu.with_memory_space_constraint(x, pltpu.HBM)
            for x in (*flat, stiff, buoy, wind.reshape(1, 128))
        ]
        result = [field(N), field(N + 4), field(N + 4), field(N + 4)]
        state = pl.pallas_call(
            lambda *refs: both_steps(ranges, heights, *refs),
            out_shape=result,
            in_specs=[pl.BlockSpec(memory_space=pltpu.HBM)] * 7,
            out_specs=[pl.BlockSpec(memory_space=pltpu.VMEM)] * 4,
            scratch_shapes=[field(64)] * 8
            + [
                field(1),
                field(1),
                pltpu.VMEM((1, 128), jnp.float32),
                messages(UP, 3, 1),
                messages(UP, 3, 1),
                messages(DOWN, 3, 0),
                messages(DOWN, 3, 0),
                pltpu.VMEM((ROWS + 2 * H, 128), jnp.float32),
                pltpu.VMEM((3, ROWS, 128), jnp.float32),
                pltpu.VMEM((16, H, 128), jnp.float32),
                field(1),
                field(1),
                pltpu.SemaphoreType.DMA((7,)),
                pltpu.SemaphoreType.DMA((10,)),
                pltpu.SemaphoreType.DMA((10,)),
                pltpu.SemaphoreType.REGULAR,
            ],
            compiler_params=pltpu.CompilerParams(
                collective_id=0, has_side_effects=True, vmem_limit_bytes=24 * 2**20
            ),
        )(*arguments)
        out = pl.pallas_call(
            store,
            out_shape=[jax.ShapeDtypeStruct((N * H, 128), jnp.float32)] * 4,
            in_specs=[pl.BlockSpec(memory_space=pltpu.VMEM)] * 4,
            out_specs=[pl.BlockSpec(memory_space=pltpu.HBM)] * 4,
            scratch_shapes=[pltpu.SemaphoreType.DMA((4,))],
            compiler_params=pltpu.CompilerParams(vmem_limit_bytes=24 * 2**20),
        )(*state)
        return tuple(x.reshape(N, H, 128) for x in out)

    field_spec = P("range", "height", None)
    return jax.shard_map(
        on_device,
        mesh=mesh,
        in_specs=(field_spec,) * 4 + (P("height", None), P("height", None), P()),
        out_specs=(field_spec,) * 4,
        check_vma=False,
    )
```

```python
import functools

import jax
import jax.numpy as jnp
from jax import lax
from jax.experimental import pallas as pl
from jax.experimental.pallas import tpu as pltpu
from jax.sharding import PartitionSpec as P

MESH = pl.DeviceIdType.MESH
N = 48
H = 8
HALO = 14
SHIFT = 8
BASE = 3
ROWS = 56
FIRST = 40
REST = ROWS - FIRST
PART = 32
UP, DOWN = 7, 6
LINE = 8


def planes(ref, start, count):
    rows = pl.ds(pl.multiple_of(start * H, H), count * H)
    return ref[rows, :].reshape(count, H, 128)


def put(ref, start, value):
    rows = pl.ds(pl.multiple_of(start * H, H), value.shape[0] * H)
    ref[rows, :] = value.reshape(value.shape[0] * H, 128)


def row(ref, start, k):
    return ref[pl.ds(start * H + k, H, stride=H), :]


def put_row(ref, start, k, value):
    ref[pl.ds(start * H + k, H, stride=H), :] = value


def lat(value, steps):
    return pltpu.roll(value, steps % 128, 2)


def hgt(value, steps):
    return pltpu.roll(value, steps % H, 1)


def central(x, count):
    return 8.0 * (x[3 : 3 + count] - x[1 : 1 + count]) - (x[4 : 4 + count] - x[0:count])


def flows(src, dst, start, count, to, coef):
    press, vert, radial, lateral = src
    new_vert, new_radial, new_lateral = dst
    p = planes(press, start - 1, count + 3)
    u = planes(radial, start - 2, count + 4)
    v = planes(lateral, start - 2, count + 4)
    w = planes(vert, start - 2, count + 4)
    b1, a1, s0, s1, k0, k1, k2, km = (coef[i] for i in range(8))
    here, mid = p[1 : 1 + count], w[2 : 2 + count]
    put(
        new_radial,
        to,
        u[2 : 2 + count]
        - b1 * (27.0 * (p[2 : 2 + count] - here) - (p[3 : 3 + count] - p[0:count]))
        - a1 * central(u, count)
        - (s0 * mid + s1 * hgt(mid, 1)),
    )
    put(
        new_lateral,
        to,
        v[2 : 2 + count]
        - b1 * (27.0 * (lat(here, -1) - here) - (lat(here, -2) - lat(here, 1)))
        - a1 * central(v, count),
    )
    put(
        new_vert,
        to,
        mid
        + (k0 * here - k1 * hgt(here, -1))
        + (k2 * hgt(here, -2) - km * hgt(here, 1))
        - a1 * central(w, count),
    )


def pressures(press, new, dst, start, at, count, to, coef):
    new_vert, new_radial, new_lateral = new
    p = planes(press, start - 2, count + 4)
    u = planes(new_radial, at - 2, count + 3)
    v = planes(new_lateral, at, count)
    w = planes(new_vert, at, count)
    c1, a1, d1, d2, dm = coef[8], coef[1], coef[9], coef[10], coef[11]
    spread = (
        27.0 * (u[2 : 2 + count] - u[1 : 1 + count])
        - (u[3 : 3 + count] - u[0:count])
        + 27.0 * (v - lat(v, 1))
        - (lat(v, -1) - lat(v, 2))
        + (27.0 * w - d1 * hgt(w, 1))
        - (dm * hgt(w, -1) - d2 * hgt(w, 2))
    )
    put(dst, to, p[2 : 2 + count] - c1 * spread - a1 * central(p, count))


def line(ref, i):
    return jnp.broadcast_to(ref[pl.ds(i, 1), :], (H, 128))


def changes(coef, low_p, high_p, high_p2):
    b24 = coef.at[0]
    return (
        -line(b24, 0) * low_p,
        line(b24, 6) * high_p,
        line(b24, 7) * (high_p2 - 27.0 * high_p),
    )


def correct_pressure(ref, at, coef, du, d0, d6, d7, low1, low2, high):
    c24 = coef.at[8]
    for i, add in (
        (0, du + 27.0 * (d0 - low1) + low2),
        (1, low1 - 27.0 * d0),
        (2, d0),
        (5, -d6),
        (6, 27.0 * d6 - d7),
        (7, 27.0 * (d7 - d6) - high),
    ):
        put_row(ref, at, i, row(ref, at, i) - line(c24, i) * add)


def add_row(ref, at, i, value):
    new = row(ref, at, i) + value
    put_row(ref, at, i, new)
    return new


def both_steps(
    ranges,
    heights,
    press_in,
    vert_in,
    radial_in,
    lateral_in,
    stiff_in,
    buoy_in,
    wind_in,
    p2,
    w2,
    u2,
    v2,
    p0,
    w0,
    u0,
    v0,
    p1,
    w1,
    u1,
    v1,
    stiff,
    buoy,
    wind,
    up_send,
    up_recv,
    down_send,
    down_recv,
    up_relay,
    down_relay,
    low_w,
    halo,
    coef,
    low_more,
    high_more,
    local_sem,
    send_sem,
    recv_sem,
    ready,
    via_ready,
):
    r, h = lax.axis_index("range"), lax.axis_index("height")
    first_r, last_r = r == 0, r == ranges - 1
    first_h, last_h = h == 0, h == heights - 1
    left = (lax.rem(r + ranges - 1, ranges), h)
    right = (lax.rem(r + 1, ranges), h)
    below = (r, lax.rem(h + heights - 1, heights))
    above = (r, lax.rem(h + 1, heights))
    no_left, no_right = jnp.logical_not(first_r), jnp.logical_not(last_r)
    no_below, no_above = jnp.logical_not(first_h), jnp.logical_not(last_h)
    odd = lax.rem(h, 2) == 1
    is_late = lax.rem(h // 2, 2) == 1
    is_early = jnp.logical_not(is_late)
    even = jnp.logical_not(odd)
    far_up, far_down = jnp.logical_and(odd, no_above), jnp.logical_and(even, no_below)
    near_up, near_down = jnp.logical_and(even, no_above), jnp.logical_and(odd, no_below)

    place = lax.rem(r, LINE)
    has_far = jnp.logical_or(far_up, far_down)
    goes_via = is_early & has_far & no_left & (place == LINE - 2)
    ends_via = is_late & has_far & no_left & (place == LINE - 2)
    relays = is_early & has_far & no_right & (place == LINE - 3)
    left_above, left_below = (left[0], above[1]), (left[0], below[1])
    right_above, right_below = (right[0], above[1]), (right[0], below[1])

    barrier = pltpu.get_barrier_semaphore()
    for there, device in (
        (no_right, right),
        (near_up, above),
        (near_down, below),
        (jnp.logical_and(is_early, far_up), above),
        (jnp.logical_and(is_early, far_down), below),
        (relays & far_up, right_above),
        (relays & far_down, right_below),
    ):

        @pl.when(there)
        def _():
            pl.semaphore_signal(barrier, inc=1, device_id=device, device_id_type=MESH)

    whole = pl.ds(0, N * H)
    loads = [
        pltpu.make_async_copy(src, dst, local_sem.at[i])
        for i, (src, dst) in enumerate(
            (
                (buoy_in, buoy),
                (stiff_in, stiff),
                (wind_in, wind),
                (press_in, p0.at[whole]),
                (vert_in, w0.at[whole]),
                (radial_in, u0.at[whole]),
                (lateral_in, v0.at[whole]),
            )
        )
    ]
    for load in loads:
        load.start()
    def remote(src, dst, i, device, sending=None):
        return pltpu.make_async_remote_copy(
            src_ref=src,
            dst_ref=dst,
            send_sem=send_sem.at[i if sending is None else sending],
            recv_sem=recv_sem.at[i],
            device_id=device,
            device_id_type=MESH,
        )

    head, tail = pl.ds(0, HALO * H), pl.ds(N * H, HALO * H)
    ups = [remote(up_send[i], up_recv[i], i, above) for i in range(3)]
    downs = [remote(down_send[i], down_recv[i], 3 + i, below) for i in range(3)]
    vias = (
        (far_up, remote(up_send[1], up_relay, 10, left)),
        (far_down, remote(down_send[1], down_relay, 10, left)),
    )
    forwards = (
        (far_up, remote(up_relay, up_recv[1], 1, right_above, 11)),
        (far_down, remote(down_relay, down_recv[1], 4, right_below, 11)),
    )
    lefts = [
        remote(src.at[head], dst.at[tail], 6 + i, left)
        for i, (src, dst) in enumerate(
            ((press_in, p0), (radial_in, u0), (vert_in, w0), (lateral_in, v0))
        )
    ]

    late_far = jnp.logical_and(is_late, jnp.logical_or(far_up, far_down))
    early_far = jnp.logical_and(is_early, jnp.logical_or(far_up, far_down))
    peers = sum(
        there.astype(jnp.int32)
        for there in (
            no_left,
            jnp.logical_or(near_up, near_down),
            late_far,
            ends_via,
        )
    )
    waits_long = jnp.logical_and(is_early, place == 0)

    def greet():
        pl.semaphore_wait(barrier, peers)
        for there, device, signal in (
            (is_late & far_up, above, ready),
            (is_late & far_down, below, ready),
            (ends_via & far_up, left_above, via_ready),
            (ends_via & far_down, left_below, via_ready),
        ):

            @pl.when(there)
            def _():
                pl.semaphore_signal(signal, inc=1, device_id=device, device_id_type=MESH)

        @pl.when(no_left)
        def _():
            for copy in lefts:
                copy.start()

    pl.when(jnp.logical_not(waits_long))(greet)

    for load in loads[:3]:
        load.wait()

    k = lax.broadcasted_iota(jnp.int32, (H, 128), 0)
    lane = lax.broadcasted_iota(jnp.int32, (H, 128), 1)
    spread_wind = jnp.broadcast_to(wind[...], (H, 128))
    top = heights * H - 1

    def wind_at(rows):
        chosen = jnp.where(lane == rows, spread_wind, 0.0)
        return jnp.broadcast_to(jnp.sum(chosen, axis=1, keepdims=True), (H, 128))

    def shear_at(rows):
        upper = wind_at(jnp.where(rows < top, rows + 1, top))
        lower = wind_at(jnp.where(rows > 0, rows - 1, 0))
        return 0.5 * (upper - lower)

    mine = k + h * H
    b24, c24 = buoy[...] * (1.0 / 24.0), stiff[...] * (1.0 / 24.0)
    a12 = wind_at(mine) * (1.0 / 12.0)
    half_shear = 0.5 * shear_at(mine)
    b27 = b24 * 27.0
    full = jnp.full((H, 128), 27.0, jnp.float32)
    one = jnp.full((H, 128), 1.0, jnp.float32)
    for i, value in enumerate(
        (
            b24,
            a12,
            half_shear,
            jnp.where(k > 0, half_shear, 0.0),
            b27,
            jnp.where(k < H - 1, b27, 0.0),
            jnp.where(k < H - 2, b24, 0.0),
            jnp.where(k > 0, b24, 0.0),
            c24,
            jnp.where(k > 0, full, 0.0),
            jnp.where(k > 1, one, 0.0),
            jnp.where(k < H - 1, one, 0.0),
        )
    ):
        coef[i] = value
    for i, outside in enumerate((-1, -2, H)):
        coef[12 + i] = wind_at(jnp.zeros_like(k) + (h * H + outside)) * (1.0 / 12.0)
    s_low = 0.5 * shear_at(jnp.zeros_like(k) + h * H)
    s_high = 0.5 * shear_at(jnp.zeros_like(k) + (h * H + H))

    def free_flows(start, step, times):
        def body(j, carry):
            at = start + step * j
            flows((p0, w0, u0, v0), (w1, u1, v1), at, step, at, coef)
            return carry

        lax.fori_loop(0, times, body, 0)

    def free_pressures(start, step, times):
        def body(j, carry):
            at = start + step * j
            pressures(p0, (w1, u1, v1), p1, at, at, step, at, coef)
            return carry

        lax.fori_loop(0, times, body, 0)

    up_rows = ((p0, 7), (w0, 7)), ((w1, 7), (w1, 6)), ((p1, 7), (p1, 6), (p1, 5))
    down_rows = ((p0, 0), (p0, 1)), ((w1, 0),), ((p1, 0), (p1, 1), (p1, 2))

    def pack(buffer, to, rows, start, count):
        def body(j, carry):
            for q, (ref, height) in enumerate(rows):
                at = pl.ds(pl.multiple_of(to + q * count + j * H, H), H)
                buffer[at, :] = row(ref, start + H * j, height)
            return carry

        lax.fori_loop(0, count // H, body, 0)

    sides = (up_send, up_rows), (down_send, down_rows)

    def send(i):
        for there, copies in ((far_up, ups), (far_down, downs)):
            pl.when(is_late & there)(copies[i].start)
        if i == 1:
            for there, copy in vias:
                pl.when(there & goes_via)(copy.start)
        for there, copies in ((near_up, ups), (near_down, downs)):
            pl.when(there)(copies[i].start)

    for load in loads[3:]:
        load.wait()
    for buffers, (given, _, _) in sides:
        pack(buffers[0], 0, given, BASE, FIRST)
    next_w = line(w0, (BASE + FIRST) * H + 7)
    for_above = jnp.where(k == 3, next_w, jnp.where(k > 3, c24, pltpu.roll(b24, 2, 0)))
    up_send[0][pl.ds(2 * FIRST, H), :] = for_above
    down_send[0][pl.ds(2 * FIRST, H), :] = jnp.where(k < 4, c24, pltpu.roll(b24, 7, 0))
    pl.when(jnp.logical_not(waits_long))(lambda: send(0))
    free_flows(BASE, 6, 7)
    free_pressures(BASE, 5, 8)
    for buffers, (_, flow_rows, press_rows) in sides:
        pack(buffers[1], 0, flow_rows, BASE, FIRST)
        pack(buffers[1], len(flow_rows) * FIRST, press_rows, SHIFT, PART)

    @pl.when(waits_long)
    def _():
        greet()
        send(0)

    send(1)

    eager = jnp.logical_and(is_early, place == LINE - 1)
    for there, outgoing in ((far_up, ups), (far_down, downs)):

        @pl.when(jnp.logical_and(there, eager))
        def _():
            pl.semaphore_wait(ready, 1)
            for copy in outgoing[:2]:
                copy.start()

    nothing = jnp.zeros((HALO * H, 128), jnp.float32)

    @pl.when(last_r)
    def _():
        for ref in (p0, u0, w0, v0):
            ref[tail, :] = nothing

    @pl.when(no_right)
    def _():
        for copy in lefts:
            copy.wait_recv()

    free_flows(45, 5, 3)

    def clear_after():
        for ref in (u1, v1, w1, p1):
            ref[pl.ds(N * H, 12 * H), :] = jnp.zeros((12 * H, 128), jnp.float32)

    pl.when(last_r)(clear_after)
    free_pressures(43, 4, 4)
    pl.when(last_r)(clear_after)
    for buffers, (given, flow_rows, press_rows) in sides:
        pack(buffers[2], 0, given + flow_rows, BASE + FIRST, REST)
        pack(buffers[2], len(given + flow_rows) * REST, press_rows, SHIFT + PART, REST)
    up_send[2][pl.ds(UP * REST, H), :] = row(w0, BASE + ROWS - H + 1, 7)
    send(2)

    for there, outgoing in ((far_up, ups), (far_down, downs)):
        pl.when(jnp.logical_and(there, eager))(outgoing[2].start)

        @pl.when(jnp.logical_and(there, jnp.logical_and(is_early, jnp.logical_not(eager))))
        def _():
            pl.semaphore_wait(ready, 1)
            outgoing[0].start()
            pl.when(jnp.logical_not(goes_via))(outgoing[1].start)
            outgoing[2].start()

    pl.when(relays)(lambda: pl.semaphore_wait(via_ready, 1))
    for (there, came), (_, copy) in zip(vias, forwards):

        @pl.when(there & relays)
        def _():
            came.wait_recv()
            copy.start()

    first_plane = jnp.where(first_r, SHIFT, 0)
    after_plane = jnp.where(last_r, N, 2 * N)

    def zero(ref, start, count):
        ref[pl.ds(start, count), :] = jnp.zeros((count, 128), jnp.float32)

    def arrived(parts):
        for none, some, copies, buffers in (
            (first_h, no_below, ups, up_recv),
            (last_h, no_above, downs, down_recv),
        ):

            @pl.when(some)
            def _():
                for i in parts:
                    copies[i].wait_recv()

            @pl.when(none)
            def _():
                for i in parts:
                    zero(buffers[i], 0, buffers[i].shape[0])

    def tile(ref, at):
        return ref[pl.ds(pl.multiple_of(at, H), H), :]

    def first_part(buffers, q, j):
        ref, at = (buffers[0], q) if q < 2 else (buffers[1], q - 2)
        return tile(ref, at * FIRST + j * H)

    def last_part(buffers, q, j):
        return tile(buffers[2], q * REST - FIRST + j * H)

    def first_pressure(buffers, flow_rows, q, j):
        return tile(buffers[1], flow_rows * FIRST + q * PART + j * H)

    def last_pressure(buffers, flow_rows, q, j):
        return tile(buffers[2], (2 + flow_rows + q) * REST - PART + j * H)

    def own_parts(at):
        own_p0, own_p1, own_p7 = row(p0, at, 0), row(p0, at, 1), row(p0, at, 7)
        return (
            line(low_more, 1) * (own_p1 - 27.0 * own_p0),
            line(low_more, 0) * own_p0,
            -line(high_more, 7) * own_p7,
        )

    def correct_first(part, j, carry):
        at = BASE + H * j
        here = pl.ds(pl.multiple_of(j * H, H), H)
        low_p0, _, low_w1, low_w2 = (part(up_recv, q, j) for q in range(4))
        high_p0, high_p1, high_w = (part(down_recv, q, j) for q in range(3))
        wl = [low_w[pl.ds(j * H + H + s, H), :] for s in (-2, -1, 0, 1)]
        e1, e2, e8 = own_parts(at)
        low_w1, low_w2, high_w = low_w1 + e1, low_w2 + e2, high_w + e8
        d0, d6, d7 = changes(coef, low_p0, high_p0, high_p1)
        for i, d in ((0, d0), (6, d6), (7, d7)):
            add_row(w1, at, i, d)
        add_row(u1, at, 0, -s_low * wl[2])
        du = -s_low * (27.0 * (wl[2] - wl[1]) - (wl[3] - wl[0]))
        correct_pressure(p1, at, coef, du, d0, d6, d7, low_w1, low_w2, high_w)
        plane = k + at
        keep = jnp.logical_and(plane >= first_plane, plane < after_plane)
        for i, value in enumerate((low_w1, low_w2, high_w)):
            halo[i, here, :] = jnp.where(keep, value, 0.0)
        return carry

    def second_flows(start, step, times):
        def body(j, carry):
            at = start + step * j
            flows((p1, w1, u1, v1), (w2, u2, v2), at + SHIFT, step, at + 2, coef)
            return carry

        lax.fori_loop(0, times, body, 0)

    def second_pressures(start, step, times):
        def body(j, carry):
            at = start + step * j
            pressures(p1, (w2, u2, v2), p2, at + SHIFT, at + 2, step, at, coef)
            return carry

        lax.fori_loop(0, times, body, 0)

    def correct_second(part, j, carry):
        at = H * j
        plane = at + SHIFT
        off = plane - BASE

        def rows_of(i, s=0):
            return halo[i, pl.ds(off + s, H), :]

        def across(i):
            return 8.0 * (rows_of(i, 1) - rows_of(i, -1)) - (rows_of(i, 2) - rows_of(i, -2))

        low_w1, low_w2, high_w = (rows_of(i) for i in range(3))
        e1, e2, e8 = own_parts(plane)
        new0, new6, new7 = (row(w1, plane, i) for i in (0, 6, 7))
        wt = [row(w0, plane + s, 7) for s in (-2, -1, 0, 1)]
        du_high = -s_high * (27.0 * (wt[2] - wt[1]) - (wt[3] - wt[0]))
        inside = k + plane < after_plane
        low_p1, low_p2, low_p3, high_p1, high_p2, high_p3 = (
            jnp.where(inside, value, 0.0)
            for value in (
                part(up_recv, 2, 0, j) - line(low_more, 7) * (27.0 * (e1 - e2) - new0),
                part(up_recv, 2, 1, j) - line(low_more, 6) * (27.0 * e2 - e1),
                part(up_recv, 2, 2, j) + line(low_more, 5) * e2,
                part(down_recv, 1, 0, j)
                - line(high_more, 0) * (du_high + 27.0 * (e8 - new7) + new6),
                part(down_recv, 1, 1, j) - line(high_more, 1) * (new7 - 27.0 * e8),
                part(down_recv, 1, 2, j) - line(high_more, 2) * e8,
            )
        )
        own_p0, own_p1, own_p7 = (row(p1, plane, i) for i in (0, 1, 7))
        d0, d6, d7 = changes(coef, low_p1, high_p1, high_p2)
        for i, d in ((0, d0), (6, d6), (7, d7)):
            add_row(w2, at + 2, i, d)
        du = -s_low * (27.0 * (low_w1 - rows_of(0, -1)) - (rows_of(0, 1) - rows_of(0, -2)))
        new1 = (
            low_w1
            - line(low_more, 1) * (27.0 * (own_p0 - low_p1) - (own_p1 - low_p2))
            - coef[12] * across(0)
        )
        new2 = (
            low_w2
            - line(low_more, 0) * (27.0 * (low_p1 - low_p2) - (own_p0 - low_p3))
            - coef[13] * across(1)
        )
        new8 = (
            high_w
            - line(high_more, 7) * (27.0 * (high_p2 - high_p1) - (high_p3 - own_p7))
            - coef[14] * across(2)
        )
        correct_pressure(p2, at, coef, du, d0, d6, d7, new1, new2, new8)
        return carry

    arrived((0, 1))
    more = pl.ds(2 * FIRST, H)
    low_more[...], high_more[...] = up_recv[0][more, :], down_recv[0][more, :]
    zero(low_w, 0, H)
    low_w[pl.ds(H, FIRST), :] = up_recv[0][pl.ds(FIRST, FIRST), :]
    low_w[pl.ds(H + FIRST, H), :] = line(low_more, 3)
    lax.fori_loop(0, FIRST // H, functools.partial(correct_first, first_part), 0)

    @pl.when(first_r)
    def _():
        for ref in (u1, v1, w1, p1):
            zero(ref, 0, SHIFT * H)

    second_flows(-2, 5, 7)
    pl.when(first_r)(lambda: zero(u2, 0, 2 * H))
    second_pressures(0, 8, PART // 8)
    lax.fori_loop(0, PART // H, functools.partial(correct_second, first_pressure), 0)

    arrived((2,))
    low_w[pl.ds(H + FIRST, REST), :] = up_recv[2][pl.ds(REST, REST), :]
    low_w[pl.ds(H + ROWS, H), :] = line(up_recv[2], UP * REST + H - 1)
    lax.fori_loop(FIRST // H, ROWS // H, functools.partial(correct_first, last_part), 0)
    pl.when(last_r)(clear_after)
    second_flows(PART + 1, 8, 2)
    second_pressures(PART, 8, (N - PART) // 8)
    lax.fori_loop(PART // H, N // H, functools.partial(correct_second, last_pressure), 0)

    def correct_radial(j, carry):
        rows = halo[0, pl.ds(H * j + SHIFT - BASE, H), :]
        add_row(u2, H * j + 2, 0, -s_low * rows)
        return carry

    lax.fori_loop(0, N // H, correct_radial, 0)

    for some, far, copies in ((no_above, far_up, ups), (no_below, far_down, downs)):

        @pl.when(some)
        def _():
            copies[0].wait_send()
            pl.when(jnp.logical_not(far & goes_via))(copies[1].wait_send)
            copies[2].wait_send()

    for there, copy in vias:
        pl.when(there & goes_via)(copy.wait_send)
    for there, copy in forwards:
        pl.when(there & relays)(copy.wait_send)

    @pl.when(no_left)
    def _():
        for copy in lefts:
            copy.wait_send()


def store(p2, w2, u2, v2, press_out, vert_out, radial_out, lateral_out, sems):
    inner = pl.ds(2 * H, N * H)
    copies = [
        pltpu.make_async_copy(src, dst, sems.at[i])
        for i, (src, dst) in enumerate(
            (
                (p2, press_out),
                (w2.at[inner], vert_out),
                (u2.at[inner], radial_out),
                (v2.at[inner], lateral_out),
            )
        )
    ]
    for copy in copies:
        copy.start()
    for copy in copies:
        copy.wait()


def solution(mesh):
    ranges, heights = mesh.shape["range"], mesh.shape["height"]

    def on_device(press, vert, radial, lateral, stiff, buoy, wind):
        def field(count):
            return pltpu.VMEM((count * H, 128), jnp.float32)

        def messages(rows, press_rows, more):
            flow_rows = rows - 2 - press_rows
            first = 2 * FIRST + H
            second = flow_rows * FIRST + press_rows * PART
            third = rows * REST + more * H
            return [pltpu.VMEM((count, 128), jnp.float32) for count in (first, second, third)]

        flat = [x.reshape(N * H, 128) for x in (press, vert, radial, lateral)]
        arguments = [
            pltpu.with_memory_space_constraint(x, pltpu.HBM)
            for x in (*flat, stiff, buoy, wind.reshape(1, 128))
        ]
        result = [field(N), field(N + 4), field(N + 4), field(N + 4)]
        state = pl.pallas_call(
            lambda *refs: both_steps(ranges, heights, *refs),
            out_shape=result,
            in_specs=[pl.BlockSpec(memory_space=pltpu.HBM)] * 7,
            out_specs=[pl.BlockSpec(memory_space=pltpu.VMEM)] * 4,
            scratch_shapes=[field(64)] * 8
            + [
                field(1),
                field(1),
                pltpu.VMEM((1, 128), jnp.float32),
                messages(UP, 3, 1),
                messages(UP, 3, 1),
                messages(DOWN, 3, 0),
                messages(DOWN, 3, 0),
                messages(UP, 3, 1)[1],
                messages(DOWN, 3, 0)[1],
                pltpu.VMEM((ROWS + 2 * H, 128), jnp.float32),
                pltpu.VMEM((3, ROWS, 128), jnp.float32),
                pltpu.VMEM((16, H, 128), jnp.float32),
                field(1),
                field(1),
                pltpu.SemaphoreType.DMA((7,)),
                pltpu.SemaphoreType.DMA((12,)),
                pltpu.SemaphoreType.DMA((11,)),
                pltpu.SemaphoreType.REGULAR,
                pltpu.SemaphoreType.REGULAR,
            ],
            compiler_params=pltpu.CompilerParams(
                collective_id=0, has_side_effects=True, vmem_limit_bytes=24 * 2**20
            ),
        )(*arguments)
        out = pl.pallas_call(
            store,
            out_shape=[jax.ShapeDtypeStruct((N * H, 128), jnp.float32)] * 4,
            in_specs=[pl.BlockSpec(memory_space=pltpu.VMEM)] * 4,
            out_specs=[pl.BlockSpec(memory_space=pltpu.HBM)] * 4,
            scratch_shapes=[pltpu.SemaphoreType.DMA((4,))],
            compiler_params=pltpu.CompilerParams(vmem_limit_bytes=24 * 2**20),
        )(*state)
        return tuple(x.reshape(N, H, 128) for x in out)

    field_spec = P("range", "height", None)
    return jax.shard_map(
        on_device,
        mesh=mesh,
        in_specs=(field_spec,) * 4 + (P("height", None), P("height", None), P()),
        out_specs=(field_spec,) * 4,
        check_vma=False,
    )
```

```python
import functools

import jax
import jax.numpy as jnp
from jax import lax
from jax.experimental import pallas as pl
from jax.experimental.pallas import tpu as pltpu
from jax.sharding import PartitionSpec as P

MESH = pl.DeviceIdType.MESH
N = 48
H = 8
HALO = 14
SHIFT = 8
BASE = 3
ROWS = 56
FIRST = 40
REST = ROWS - FIRST
PART = 32
UP, DOWN = 7, 6
LINE = 8


def planes(ref, start, count):
    rows = pl.ds(pl.multiple_of(start * H, H), count * H)
    return ref[rows, :].reshape(count, H, 128)


def put(ref, start, value):
    rows = pl.ds(pl.multiple_of(start * H, H), value.shape[0] * H)
    ref[rows, :] = value.reshape(value.shape[0] * H, 128)


def row(ref, start, k):
    return ref[pl.ds(start * H + k, H, stride=H), :]


def put_row(ref, start, k, value):
    ref[pl.ds(start * H + k, H, stride=H), :] = value


def lat(value, steps):
    return pltpu.roll(value, steps % 128, 2)


def hgt(value, steps):
    return pltpu.roll(value, steps % H, 1)


def central(x, count):
    return 8.0 * (x[3 : 3 + count] - x[1 : 1 + count]) - (x[4 : 4 + count] - x[0:count])


def flows(src, dst, start, count, to, coef):
    press, vert, radial, lateral = src
    new_vert, new_radial, new_lateral = dst
    p = planes(press, start - 1, count + 3)
    u = planes(radial, start - 2, count + 4)
    v = planes(lateral, start - 2, count + 4)
    w = planes(vert, start - 2, count + 4)
    b1, a1, s0, s1, k0, k1, k2, km = (coef[i] for i in range(8))
    here, mid = p[1 : 1 + count], w[2 : 2 + count]
    put(
        new_radial,
        to,
        u[2 : 2 + count]
        - b1 * (27.0 * (p[2 : 2 + count] - here) - (p[3 : 3 + count] - p[0:count]))
        - a1 * central(u, count)
        - (s0 * mid + s1 * hgt(mid, 1)),
    )
    put(
        new_lateral,
        to,
        v[2 : 2 + count]
        - b1 * (27.0 * (lat(here, -1) - here) - (lat(here, -2) - lat(here, 1)))
        - a1 * central(v, count),
    )
    put(
        new_vert,
        to,
        mid
        + (k0 * here - k1 * hgt(here, -1))
        + (k2 * hgt(here, -2) - km * hgt(here, 1))
        - a1 * central(w, count),
    )


def pressures(press, new, dst, start, at, count, to, coef):
    new_vert, new_radial, new_lateral = new
    p = planes(press, start - 2, count + 4)
    u = planes(new_radial, at - 2, count + 3)
    v = planes(new_lateral, at, count)
    w = planes(new_vert, at, count)
    c1, a1, d1, d2, dm = coef[8], coef[1], coef[9], coef[10], coef[11]
    spread = (
        27.0 * (u[2 : 2 + count] - u[1 : 1 + count])
        - (u[3 : 3 + count] - u[0:count])
        + 27.0 * (v - lat(v, 1))
        - (lat(v, -1) - lat(v, 2))
        + (27.0 * w - d1 * hgt(w, 1))
        - (dm * hgt(w, -1) - d2 * hgt(w, 2))
    )
    put(dst, to, p[2 : 2 + count] - c1 * spread - a1 * central(p, count))


def line(ref, i):
    return jnp.broadcast_to(ref[pl.ds(i, 1), :], (H, 128))


def changes(coef, low_p, high_p, high_p2):
    b24 = coef.at[0]
    return (
        -line(b24, 0) * low_p,
        line(b24, 6) * high_p,
        line(b24, 7) * (high_p2 - 27.0 * high_p),
    )


def correct_pressure(ref, at, coef, du, d0, d6, d7, low1, low2, high):
    c24 = coef.at[8]
    for i, add in (
        (0, du + 27.0 * (d0 - low1) + low2),
        (1, low1 - 27.0 * d0),
        (2, d0),
        (5, -d6),
        (6, 27.0 * d6 - d7),
        (7, 27.0 * (d7 - d6) - high),
    ):
        put_row(ref, at, i, row(ref, at, i) - line(c24, i) * add)


def add_row(ref, at, i, value):
    new = row(ref, at, i) + value
    put_row(ref, at, i, new)
    return new


def both_steps(
    ranges,
    heights,
    press_in,
    vert_in,
    radial_in,
    lateral_in,
    stiff_in,
    buoy_in,
    wind_in,
    p2,
    w2,
    u2,
    v2,
    p0,
    w0,
    u0,
    v0,
    p1,
    w1,
    u1,
    v1,
    stiff,
    buoy,
    wind,
    up_send,
    up_recv,
    down_send,
    down_recv,
    up_relay,
    down_relay,
    low_w,
    halo,
    coef,
    low_more,
    high_more,
    local_sem,
    send_sem,
    recv_sem,
    ready,
    via_ready,
):
    r, h = lax.axis_index("range"), lax.axis_index("height")
    first_r, last_r = r == 0, r == ranges - 1
    first_h, last_h = h == 0, h == heights - 1
    left = (lax.rem(r + ranges - 1, ranges), h)
    right = (lax.rem(r + 1, ranges), h)
    below = (r, lax.rem(h + heights - 1, heights))
    above = (r, lax.rem(h + 1, heights))
    no_left, no_right = jnp.logical_not(first_r), jnp.logical_not(last_r)
    no_below, no_above = jnp.logical_not(first_h), jnp.logical_not(last_h)
    odd = lax.rem(h, 2) == 1
    is_late = lax.rem(h // 2, 2) == 1
    is_early = jnp.logical_not(is_late)
    even = jnp.logical_not(odd)
    far_up, far_down = jnp.logical_and(odd, no_above), jnp.logical_and(even, no_below)
    near_up, near_down = jnp.logical_and(even, no_above), jnp.logical_and(odd, no_below)

    place = lax.rem(r, LINE)
    has_far = jnp.logical_or(far_up, far_down)
    goes_via = is_early & has_far & no_left & (place == LINE - 2)
    ends_via = is_late & has_far & no_left & (place == LINE - 2)
    relays = is_early & has_far & no_right & (place == LINE - 3)
    left_above, left_below = (left[0], above[1]), (left[0], below[1])
    right_above, right_below = (right[0], above[1]), (right[0], below[1])

    barrier = pltpu.get_barrier_semaphore()
    for there, device in (
        (no_right, right),
        (near_up, above),
        (near_down, below),
        (jnp.logical_and(is_early, far_up), above),
        (jnp.logical_and(is_early, far_down), below),
        (relays & far_up, right_above),
        (relays & far_down, right_below),
    ):

        @pl.when(there)
        def _():
            pl.semaphore_signal(barrier, inc=1, device_id=device, device_id_type=MESH)

    whole = pl.ds(0, N * H)
    loads = [
        pltpu.make_async_copy(src, dst, local_sem.at[i])
        for i, (src, dst) in enumerate(
            (
                (buoy_in, buoy),
                (stiff_in, stiff),
                (wind_in, wind),
                (press_in, p0.at[whole]),
                (vert_in, w0.at[whole]),
                (radial_in, u0.at[whole]),
                (lateral_in, v0.at[whole]),
            )
        )
    ]
    for load in loads:
        load.start()
    def remote(src, dst, i, device, sending=None):
        return pltpu.make_async_remote_copy(
            src_ref=src,
            dst_ref=dst,
            send_sem=send_sem.at[i if sending is None else sending],
            recv_sem=recv_sem.at[i],
            device_id=device,
            device_id_type=MESH,
        )

    tail = pl.ds(N * H, HALO * H)
    ups = [remote(up_send[i], up_recv[i], i, above) for i in range(3)]
    downs = [remote(down_send[i], down_recv[i], 3 + i, below) for i in range(3)]
    vias = (
        (far_up, remote(up_send[1], up_relay, 10, left)),
        (far_down, remote(down_send[1], down_relay, 10, left)),
    )
    forwards = (
        (far_up, remote(up_relay, up_recv[1], 1, right_above, 11)),
        (far_down, remote(down_relay, down_recv[1], 4, right_below, 11)),
    )
    lefts = [
        remote(src.at[pl.ds(0, count * H)], dst.at[pl.ds(N * H, count * H)], 6 + i, left)
        for i, (src, dst, count) in enumerate(
            (
                (press_in, p0, HALO),
                (radial_in, u0, HALO),
                (vert_in, w0, HALO - 1),
                (lateral_in, v0, HALO - 1),
            )
        )
    ]

    late_far = jnp.logical_and(is_late, jnp.logical_or(far_up, far_down))
    early_far = jnp.logical_and(is_early, jnp.logical_or(far_up, far_down))
    peers = sum(
        there.astype(jnp.int32)
        for there in (
            no_left,
            jnp.logical_or(near_up, near_down),
            late_far,
            ends_via,
        )
    )
    waits_long = jnp.logical_and(is_early, place == 0)

    def greet():
        pl.semaphore_wait(barrier, peers)
        for there, device, signal in (
            (is_late & far_up, above, ready),
            (is_late & far_down, below, ready),
            (ends_via & far_up, left_above, via_ready),
            (ends_via & far_down, left_below, via_ready),
        ):

            @pl.when(there)
            def _():
                pl.semaphore_signal(signal, inc=1, device_id=device, device_id_type=MESH)

        @pl.when(no_left)
        def _():
            for copy in lefts:
                copy.start()

    pl.when(jnp.logical_not(waits_long))(greet)

    for load in loads[:3]:
        load.wait()

    k = lax.broadcasted_iota(jnp.int32, (H, 128), 0)
    lane = lax.broadcasted_iota(jnp.int32, (H, 128), 1)
    spread_wind = jnp.broadcast_to(wind[...], (H, 128))
    top = heights * H - 1

    def wind_at(rows):
        chosen = jnp.where(lane == rows, spread_wind, 0.0)
        return jnp.broadcast_to(jnp.sum(chosen, axis=1, keepdims=True), (H, 128))

    def shear_at(rows):
        upper = wind_at(jnp.where(rows < top, rows + 1, top))
        lower = wind_at(jnp.where(rows > 0, rows - 1, 0))
        return 0.5 * (upper - lower)

    mine = k + h * H
    b24, c24 = buoy[...] * (1.0 / 24.0), stiff[...] * (1.0 / 24.0)
    a12 = wind_at(mine) * (1.0 / 12.0)
    half_shear = 0.5 * shear_at(mine)
    b27 = b24 * 27.0
    full = jnp.full((H, 128), 27.0, jnp.float32)
    one = jnp.full((H, 128), 1.0, jnp.float32)
    for i, value in enumerate(
        (
            b24,
            a12,
            half_shear,
            jnp.where(k > 0, half_shear, 0.0),
            b27,
            jnp.where(k < H - 1, b27, 0.0),
            jnp.where(k < H - 2, b24, 0.0),
            jnp.where(k > 0, b24, 0.0),
            c24,
            jnp.where(k > 0, full, 0.0),
            jnp.where(k > 1, one, 0.0),
            jnp.where(k < H - 1, one, 0.0),
        )
    ):
        coef[i] = value
    for i, outside in enumerate((-1, -2, H)):
        coef[12 + i] = wind_at(jnp.zeros_like(k) + (h * H + outside)) * (1.0 / 12.0)
    s_low = 0.5 * shear_at(jnp.zeros_like(k) + h * H)
    s_high = 0.5 * shear_at(jnp.zeros_like(k) + (h * H + H))

    def free_flows(start, step, times):
        def body(j, carry):
            at = start + step * j
            flows((p0, w0, u0, v0), (w1, u1, v1), at, step, at, coef)
            return carry

        lax.fori_loop(0, times, body, 0)

    def free_pressures(start, step, times):
        def body(j, carry):
            at = start + step * j
            pressures(p0, (w1, u1, v1), p1, at, at, step, at, coef)
            return carry

        lax.fori_loop(0, times, body, 0)

    up_rows = (
        ((p0, 7, 0), (w0, 7, 1)),
        ((w1, 7, 0), (w1, 6, 0)),
        ((p1, 7, 0), (p1, 6, 0), (p1, 5, 0)),
    )
    down_rows = (
        ((p0, 0, 0), (p0, 1, 0)),
        ((w1, 0, 0),),
        ((p1, 0, 0), (p1, 1, 0), (p1, 2, 0)),
    )

    def pack(buffer, to, rows, start, count):
        def body(j, carry):
            for q, (ref, height, later) in enumerate(rows):
                at = pl.ds(pl.multiple_of(to + q * count + j * H, H), H)
                buffer[at, :] = row(ref, start + later + H * j, height)
            return carry

        lax.fori_loop(0, count // H, body, 0)

    sides = (up_send, up_rows), (down_send, down_rows)

    def send(i):
        for there, copies in ((far_up, ups), (far_down, downs)):
            pl.when(is_late & there)(copies[i].start)
        if i == 1:
            for there, copy in vias:
                pl.when(there & goes_via)(copy.start)
        for there, copies in ((near_up, ups), (near_down, downs)):
            pl.when(there)(copies[i].start)

    for load in loads[3:]:
        load.wait()
    for buffers, (given, _, _) in sides:
        pack(buffers[0], 0, given, BASE, FIRST)
    first_w = line(w0, BASE * H + 7)
    for_above = jnp.where(k == 3, first_w, jnp.where(k > 3, c24, pltpu.roll(b24, 2, 0)))
    up_send[0][pl.ds(2 * FIRST, H), :] = for_above
    down_send[0][pl.ds(2 * FIRST, H), :] = jnp.where(k < 4, c24, pltpu.roll(b24, 7, 0))
    pl.when(jnp.logical_not(waits_long))(lambda: send(0))
    free_flows(BASE, 6, 7)
    free_pressures(BASE, 5, 8)
    for buffers, (_, flow_rows, press_rows) in sides:
        pack(buffers[1], 0, flow_rows, BASE, FIRST)
        pack(buffers[1], len(flow_rows) * FIRST, press_rows, SHIFT, PART)

    @pl.when(waits_long)
    def _():
        greet()
        send(0)

    send(1)

    eager = jnp.logical_and(is_early, place == LINE - 1)
    for there, outgoing in ((far_up, ups), (far_down, downs)):

        @pl.when(jnp.logical_and(there, eager))
        def _():
            pl.semaphore_wait(ready, 1)
            for copy in outgoing[:2]:
                copy.start()

    nothing = jnp.zeros((HALO * H, 128), jnp.float32)

    @pl.when(last_r)
    def _():
        for ref in (p0, u0, w0, v0):
            ref[tail, :] = nothing

    @pl.when(no_right)
    def _():
        for copy in lefts:
            copy.wait_recv()

    free_flows(45, 5, 3)

    def clear_after():
        for ref in (u1, v1, w1, p1):
            ref[pl.ds(N * H, 12 * H), :] = jnp.zeros((12 * H, 128), jnp.float32)

    pl.when(last_r)(clear_after)
    free_pressures(43, 4, 4)
    pl.when(last_r)(clear_after)
    for buffers, (given, flow_rows, press_rows) in sides:
        pack(buffers[2], 0, given + flow_rows, BASE + FIRST, REST)
        pack(buffers[2], len(given + flow_rows) * REST, press_rows, SHIFT + PART, REST)
    send(2)

    for there, outgoing in ((far_up, ups), (far_down, downs)):
        pl.when(jnp.logical_and(there, eager))(outgoing[2].start)

        @pl.when(jnp.logical_and(there, jnp.logical_and(is_early, jnp.logical_not(eager))))
        def _():
            pl.semaphore_wait(ready, 1)
            outgoing[0].start()
            pl.when(jnp.logical_not(goes_via))(outgoing[1].start)
            outgoing[2].start()

    pl.when(relays)(lambda: pl.semaphore_wait(via_ready, 1))
    for (there, came), (_, copy) in zip(vias, forwards):

        @pl.when(there & relays)
        def _():
            came.wait_recv()
            copy.start()

    first_plane = jnp.where(first_r, SHIFT, 0)
    after_plane = jnp.where(last_r, N, 2 * N)

    def zero(ref, start, count):
        ref[pl.ds(start, count), :] = jnp.zeros((count, 128), jnp.float32)

    def arrived(parts):
        for none, some, copies, buffers in (
            (first_h, no_below, ups, up_recv),
            (last_h, no_above, downs, down_recv),
        ):

            @pl.when(some)
            def _():
                for i in parts:
                    copies[i].wait_recv()

            @pl.when(none)
            def _():
                for i in parts:
                    zero(buffers[i], 0, buffers[i].shape[0])

    def tile(ref, at):
        return ref[pl.ds(pl.multiple_of(at, H), H), :]

    def first_part(buffers, q, j):
        ref, at = (buffers[0], q) if q < 2 else (buffers[1], q - 2)
        return tile(ref, at * FIRST + j * H)

    def last_part(buffers, q, j):
        return tile(buffers[2], q * REST - FIRST + j * H)

    def first_pressure(buffers, flow_rows, q, j):
        return tile(buffers[1], flow_rows * FIRST + q * PART + j * H)

    def last_pressure(buffers, flow_rows, q, j):
        return tile(buffers[2], (2 + flow_rows + q) * REST - PART + j * H)

    def own_parts(at):
        own_p0, own_p1, own_p7 = row(p0, at, 0), row(p0, at, 1), row(p0, at, 7)
        return (
            line(low_more, 1) * (own_p1 - 27.0 * own_p0),
            line(low_more, 0) * own_p0,
            -line(high_more, 7) * own_p7,
        )

    def correct_first(part, j, carry):
        at = BASE + H * j
        here = pl.ds(pl.multiple_of(j * H, H), H)
        low_p0, _, low_w1, low_w2 = (part(up_recv, q, j) for q in range(4))
        high_p0, high_p1, high_w = (part(down_recv, q, j) for q in range(3))
        wl = [low_w[pl.ds(j * H + H + s, H), :] for s in (-2, -1, 0, 1)]
        e1, e2, e8 = own_parts(at)
        low_w1, low_w2, high_w = low_w1 + e1, low_w2 + e2, high_w + e8
        d0, d6, d7 = changes(coef, low_p0, high_p0, high_p1)
        for i, d in ((0, d0), (6, d6), (7, d7)):
            add_row(w1, at, i, d)
        add_row(u1, at, 0, -s_low * wl[2])
        du = -s_low * (27.0 * (wl[2] - wl[1]) - (wl[3] - wl[0]))
        correct_pressure(p1, at, coef, du, d0, d6, d7, low_w1, low_w2, high_w)
        plane = k + at
        keep = jnp.logical_and(plane >= first_plane, plane < after_plane)
        for i, value in enumerate((low_w1, low_w2, high_w)):
            halo[i, here, :] = jnp.where(keep, value, 0.0)
        return carry

    def second_flows(start, step, times):
        def body(j, carry):
            at = start + step * j
            flows((p1, w1, u1, v1), (w2, u2, v2), at + SHIFT, step, at + 2, coef)
            return carry

        lax.fori_loop(0, times, body, 0)

    def second_pressures(start, step, times):
        def body(j, carry):
            at = start + step * j
            pressures(p1, (w2, u2, v2), p2, at + SHIFT, at + 2, step, at, coef)
            return carry

        lax.fori_loop(0, times, body, 0)

    def correct_second(part, j, carry):
        at = H * j
        plane = at + SHIFT
        off = plane - BASE

        def rows_of(i, s=0):
            return halo[i, pl.ds(off + s, H), :]

        def across(i):
            return 8.0 * (rows_of(i, 1) - rows_of(i, -1)) - (rows_of(i, 2) - rows_of(i, -2))

        low_w1, low_w2, high_w = (rows_of(i) for i in range(3))
        e1, e2, e8 = own_parts(plane)
        new0, new6, new7 = (row(w1, plane, i) for i in (0, 6, 7))
        wt = [row(w0, plane + s, 7) for s in (-2, -1, 0, 1)]
        du_high = -s_high * (27.0 * (wt[2] - wt[1]) - (wt[3] - wt[0]))
        inside = k + plane < after_plane
        low_p1, low_p2, low_p3, high_p1, high_p2, high_p3 = (
            jnp.where(inside, value, 0.0)
            for value in (
                part(up_recv, 2, 0, j) - line(low_more, 7) * (27.0 * (e1 - e2) - new0),
                part(up_recv, 2, 1, j) - line(low_more, 6) * (27.0 * e2 - e1),
                part(up_recv, 2, 2, j) + line(low_more, 5) * e2,
                part(down_recv, 1, 0, j)
                - line(high_more, 0) * (du_high + 27.0 * (e8 - new7) + new6),
                part(down_recv, 1, 1, j) - line(high_more, 1) * (new7 - 27.0 * e8),
                part(down_recv, 1, 2, j) - line(high_more, 2) * e8,
            )
        )
        own_p0, own_p1, own_p7 = (row(p1, plane, i) for i in (0, 1, 7))
        d0, d6, d7 = changes(coef, low_p1, high_p1, high_p2)
        for i, d in ((0, d0), (6, d6), (7, d7)):
            add_row(w2, at + 2, i, d)
        du = -s_low * (27.0 * (low_w1 - rows_of(0, -1)) - (rows_of(0, 1) - rows_of(0, -2)))
        new1 = (
            low_w1
            - line(low_more, 1) * (27.0 * (own_p0 - low_p1) - (own_p1 - low_p2))
            - coef[12] * across(0)
        )
        new2 = (
            low_w2
            - line(low_more, 0) * (27.0 * (low_p1 - low_p2) - (own_p0 - low_p3))
            - coef[13] * across(1)
        )
        new8 = (
            high_w
            - line(high_more, 7) * (27.0 * (high_p2 - high_p1) - (high_p3 - own_p7))
            - coef[14] * across(2)
        )
        correct_pressure(p2, at, coef, du, d0, d6, d7, new1, new2, new8)
        return carry

    arrived((0, 1))
    more = pl.ds(2 * FIRST, H)
    low_more[...], high_more[...] = up_recv[0][more, :], down_recv[0][more, :]
    zero(low_w, 0, H)
    low_w[pl.ds(H, 1), :] = low_more[pl.ds(3, 1), :]
    low_w[pl.ds(H + 1, FIRST), :] = up_recv[0][pl.ds(FIRST, FIRST), :]
    lax.fori_loop(0, FIRST // H, functools.partial(correct_first, first_part), 0)

    @pl.when(first_r)
    def _():
        for ref in (u1, v1, w1, p1):
            zero(ref, 0, SHIFT * H)

    second_flows(-2, 5, 7)
    pl.when(first_r)(lambda: zero(u2, 0, 2 * H))
    second_pressures(0, 8, PART // 8)
    lax.fori_loop(0, PART // H, functools.partial(correct_second, first_pressure), 0)

    arrived((2,))
    low_w[pl.ds(H + 1 + FIRST, REST), :] = up_recv[2][pl.ds(REST, REST), :]
    lax.fori_loop(FIRST // H, ROWS // H, functools.partial(correct_first, last_part), 0)
    pl.when(last_r)(clear_after)
    second_flows(PART + 1, 8, 2)
    second_pressures(PART, 8, (N - PART) // 8)
    lax.fori_loop(PART // H, N // H, functools.partial(correct_second, last_pressure), 0)

    def correct_radial(j, carry):
        rows = halo[0, pl.ds(H * j + SHIFT - BASE, H), :]
        add_row(u2, H * j + 2, 0, -s_low * rows)
        return carry

    lax.fori_loop(0, N // H, correct_radial, 0)

    for some, far, copies in ((no_above, far_up, ups), (no_below, far_down, downs)):

        @pl.when(some)
        def _():
            copies[0].wait_send()
            pl.when(jnp.logical_not(far & goes_via))(copies[1].wait_send)
            copies[2].wait_send()

    for there, copy in vias:
        pl.when(there & goes_via)(copy.wait_send)
    for there, copy in forwards:
        pl.when(there & relays)(copy.wait_send)

    @pl.when(no_left)
    def _():
        for copy in lefts:
            copy.wait_send()


def store(p2, w2, u2, v2, press_out, vert_out, radial_out, lateral_out, sems):
    inner = pl.ds(2 * H, N * H)
    copies = [
        pltpu.make_async_copy(src, dst, sems.at[i])
        for i, (src, dst) in enumerate(
            (
                (p2, press_out),
                (w2.at[inner], vert_out),
                (u2.at[inner], radial_out),
                (v2.at[inner], lateral_out),
            )
        )
    ]
    for copy in copies:
        copy.start()
    for copy in copies:
        copy.wait()


def solution(mesh):
    ranges, heights = mesh.shape["range"], mesh.shape["height"]

    def on_device(press, vert, radial, lateral, stiff, buoy, wind):
        def field(count):
            return pltpu.VMEM((count * H, 128), jnp.float32)

        def messages(rows, press_rows):
            flow_rows = rows - 2 - press_rows
            first = 2 * FIRST + H
            second = flow_rows * FIRST + press_rows * PART
            third = rows * REST
            return [pltpu.VMEM((count, 128), jnp.float32) for count in (first, second, third)]

        flat = [x.reshape(N * H, 128) for x in (press, vert, radial, lateral)]
        arguments = [
            pltpu.with_memory_space_constraint(x, pltpu.HBM)
            for x in (*flat, stiff, buoy, wind.reshape(1, 128))
        ]
        result = [field(N), field(N + 4), field(N + 4), field(N + 4)]
        state = pl.pallas_call(
            lambda *refs: both_steps(ranges, heights, *refs),
            out_shape=result,
            in_specs=[pl.BlockSpec(memory_space=pltpu.HBM)] * 7,
            out_specs=[pl.BlockSpec(memory_space=pltpu.VMEM)] * 4,
            scratch_shapes=[field(64)] * 8
            + [
                field(1),
                field(1),
                pltpu.VMEM((1, 128), jnp.float32),
                messages(UP, 3),
                messages(UP, 3),
                messages(DOWN, 3),
                messages(DOWN, 3),
                messages(UP, 3)[1],
                messages(DOWN, 3)[1],
                pltpu.VMEM((ROWS + 2 * H, 128), jnp.float32),
                pltpu.VMEM((3, ROWS, 128), jnp.float32),
                pltpu.VMEM((16, H, 128), jnp.float32),
                field(1),
                field(1),
                pltpu.SemaphoreType.DMA((7,)),
                pltpu.SemaphoreType.DMA((12,)),
                pltpu.SemaphoreType.DMA((11,)),
                pltpu.SemaphoreType.REGULAR,
                pltpu.SemaphoreType.REGULAR,
            ],
            compiler_params=pltpu.CompilerParams(
                collective_id=0, has_side_effects=True, vmem_limit_bytes=24 * 2**20
            ),
        )(*arguments)
        out = pl.pallas_call(
            store,
            out_shape=[jax.ShapeDtypeStruct((N * H, 128), jnp.float32)] * 4,
            in_specs=[pl.BlockSpec(memory_space=pltpu.VMEM)] * 4,
            out_specs=[pl.BlockSpec(memory_space=pltpu.HBM)] * 4,
            scratch_shapes=[pltpu.SemaphoreType.DMA((4,))],
            compiler_params=pltpu.CompilerParams(vmem_limit_bytes=24 * 2**20),
        )(*state)
        return tuple(x.reshape(N, H, 128) for x in out)

    field_spec = P("range", "height", None)
    return jax.shard_map(
        on_device,
        mesh=mesh,
        in_specs=(field_spec,) * 4 + (P("height", None), P("height", None), P()),
        out_specs=(field_spec,) * 4,
        check_vma=False,
    )
```

```python
import functools
from collections.abc import Callable
from typing import NamedTuple

import jax
import jax.numpy as jnp
from jax import lax
from jax.experimental import pallas as pl
from jax.experimental.pallas import tpu as pltpu
from jax.sharding import PartitionSpec as P

MESH = pl.DeviceIdType.MESH
N = 48
H = 8
HALO = 14
SHIFT = 8
BASE = 3
ROWS = 56
FIRST = 40
REST = ROWS - FIRST
PART = 32
UP, DOWN = 7, 6
LINE = 8


def planes(ref, start, count):
    rows = pl.ds(pl.multiple_of(start * H, H), count * H)
    return ref[rows, :].reshape(count, H, 128)


def put(ref, start, value):
    rows = pl.ds(pl.multiple_of(start * H, H), value.shape[0] * H)
    ref[rows, :] = value.reshape(value.shape[0] * H, 128)


def row(ref, start, k):
    return ref[pl.ds(start * H + k, H, stride=H), :]


def put_row(ref, start, k, value):
    ref[pl.ds(start * H + k, H, stride=H), :] = value


def lat(value, steps):
    return pltpu.roll(value, steps % 128, 2)


def hgt(value, steps):
    return pltpu.roll(value, steps % H, 1)


def central(x, count):
    return 8.0 * (x[3 : 3 + count] - x[1 : 1 + count]) - (x[4 : 4 + count] - x[0:count])


def flows(src, dst, start, count, to, coef):
    press, vert, radial, lateral = src
    new_vert, new_radial, new_lateral = dst
    p = planes(press, start - 1, count + 3)
    u = planes(radial, start - 2, count + 4)
    v = planes(lateral, start - 2, count + 4)
    w = planes(vert, start - 2, count + 4)
    b1, a1, s0, s1, k0, k1, k2, km = (coef[i] for i in range(8))
    here, mid = p[1 : 1 + count], w[2 : 2 + count]
    put(
        new_radial,
        to,
        u[2 : 2 + count]
        - b1 * (27.0 * (p[2 : 2 + count] - here) - (p[3 : 3 + count] - p[0:count]))
        - a1 * central(u, count)
        - (s0 * mid + s1 * hgt(mid, 1)),
    )
    put(
        new_lateral,
        to,
        v[2 : 2 + count]
        - b1 * (27.0 * (lat(here, -1) - here) - (lat(here, -2) - lat(here, 1)))
        - a1 * central(v, count),
    )
    put(
        new_vert,
        to,
        mid
        + (k0 * here - k1 * hgt(here, -1))
        + (k2 * hgt(here, -2) - km * hgt(here, 1))
        - a1 * central(w, count),
    )


def pressures(press, new, dst, start, at, count, to, coef):
    new_vert, new_radial, new_lateral = new
    p = planes(press, start - 2, count + 4)
    u = planes(new_radial, at - 2, count + 3)
    v = planes(new_lateral, at, count)
    w = planes(new_vert, at, count)
    c1, a1, d1, d2, dm = coef[8], coef[1], coef[9], coef[10], coef[11]
    spread = (
        27.0 * (u[2 : 2 + count] - u[1 : 1 + count])
        - (u[3 : 3 + count] - u[0:count])
        + 27.0 * (v - lat(v, 1))
        - (lat(v, -1) - lat(v, 2))
        + (27.0 * w - d1 * hgt(w, 1))
        - (dm * hgt(w, -1) - d2 * hgt(w, 2))
    )
    put(dst, to, p[2 : 2 + count] - c1 * spread - a1 * central(p, count))


def line(ref, i):
    return jnp.broadcast_to(ref[pl.ds(i, 1), :], (H, 128))


def changes(coef, low_p, high_p, high_p2):
    b24 = coef.at[0]
    return (
        -line(b24, 0) * low_p,
        line(b24, 6) * high_p,
        line(b24, 7) * (high_p2 - 27.0 * high_p),
    )


def correct_pressure(ref, at, coef, du, d0, d6, d7, low1, low2, high):
    c24 = coef.at[8]
    for i, add in (
        (0, du + 27.0 * (d0 - low1) + low2),
        (1, low1 - 27.0 * d0),
        (2, d0),
        (5, -d6),
        (6, 27.0 * d6 - d7),
        (7, 27.0 * (d7 - d6) - high),
    ):
        put_row(ref, at, i, row(ref, at, i) - line(c24, i) * add)


def add_row(ref, at, i, value):
    new = row(ref, at, i) + value
    put_row(ref, at, i, new)
    return new


def zero(ref, start, count):
    ref[pl.ds(start, count), :] = jnp.zeros((count, 128), jnp.float32)


class Finish(NamedTuple):
    first: Callable
    last: Callable
    radial: Callable


def finishing(
    ranges, p0, w0, p1, w1, u1, v1, p2, w2, u2, v2, up_recv, down_recv, low_w, halo, coef, low_more, high_more
):
    r = lax.axis_index("range")
    first_r, last_r = r == 0, r == ranges - 1
    k = lax.broadcasted_iota(jnp.int32, (H, 128), 0)
    first_plane = jnp.where(first_r, SHIFT, 0)
    after_plane = jnp.where(last_r, N, 2 * N)
    s_low, s_high = coef[15], coef[16]

    def clear_after():
        for ref in (u1, v1, w1, p1):
            zero(ref, N * H, 12 * H)

    def tile(ref, at):
        return ref[pl.ds(pl.multiple_of(at, H), H), :]

    def first_part(buffers, q, j):
        ref, at = (buffers[0], q) if q < 2 else (buffers[1], q - 2)
        return tile(ref, at * FIRST + j * H)

    def last_part(buffers, q, j):
        return tile(buffers[2], q * REST - FIRST + j * H)

    def first_pressure(buffers, flow_rows, q, j):
        return tile(buffers[1], flow_rows * FIRST + q * PART + j * H)

    def last_pressure(buffers, flow_rows, q, j):
        return tile(buffers[2], (2 + flow_rows + q) * REST - PART + j * H)

    def own_parts(at):
        own_p0, own_p1, own_p7 = row(p0, at, 0), row(p0, at, 1), row(p0, at, 7)
        return (
            line(low_more, 1) * (own_p1 - 27.0 * own_p0),
            line(low_more, 0) * own_p0,
            -line(high_more, 7) * own_p7,
        )

    def correct_first(part, j, carry):
        at = BASE + H * j
        here = pl.ds(pl.multiple_of(j * H, H), H)
        low_p0, _, low_w1, low_w2 = (part(up_recv, q, j) for q in range(4))
        high_p0, high_p1, high_w = (part(down_recv, q, j) for q in range(3))
        wl = [low_w[pl.ds(j * H + H + s, H), :] for s in (-2, -1, 0, 1)]
        e1, e2, e8 = own_parts(at)
        low_w1, low_w2, high_w = low_w1 + e1, low_w2 + e2, high_w + e8
        d0, d6, d7 = changes(coef, low_p0, high_p0, high_p1)
        for i, d in ((0, d0), (6, d6), (7, d7)):
            add_row(w1, at, i, d)
        add_row(u1, at, 0, -s_low * wl[2])
        du = -s_low * (27.0 * (wl[2] - wl[1]) - (wl[3] - wl[0]))
        correct_pressure(p1, at, coef, du, d0, d6, d7, low_w1, low_w2, high_w)
        plane = k + at
        keep = jnp.logical_and(plane >= first_plane, plane < after_plane)
        for i, value in enumerate((low_w1, low_w2, high_w)):
            halo[i, here, :] = jnp.where(keep, value, 0.0)
        return carry

    def second_flows(start, step, times):
        def body(j, carry):
            at = start + step * j
            flows((p1, w1, u1, v1), (w2, u2, v2), at + SHIFT, step, at + 2, coef)
            return carry

        lax.fori_loop(0, times, body, 0)

    def second_pressures(start, step, times):
        def body(j, carry):
            at = start + step * j
            pressures(p1, (w2, u2, v2), p2, at + SHIFT, at + 2, step, at, coef)
            return carry

        lax.fori_loop(0, times, body, 0)

    def correct_second(part, j, carry):
        at = H * j
        plane = at + SHIFT
        off = plane - BASE

        def rows_of(i, s=0):
            return halo[i, pl.ds(off + s, H), :]

        def across(i):
            return 8.0 * (rows_of(i, 1) - rows_of(i, -1)) - (rows_of(i, 2) - rows_of(i, -2))

        low_w1, low_w2, high_w = (rows_of(i) for i in range(3))
        e1, e2, e8 = own_parts(plane)
        new0, new6, new7 = (row(w1, plane, i) for i in (0, 6, 7))
        wt = [row(w0, plane + s, 7) for s in (-2, -1, 0, 1)]
        du_high = -s_high * (27.0 * (wt[2] - wt[1]) - (wt[3] - wt[0]))
        inside = k + plane < after_plane
        low_p1, low_p2, low_p3, high_p1, high_p2, high_p3 = (
            jnp.where(inside, value, 0.0)
            for value in (
                part(up_recv, 2, 0, j) - line(low_more, 7) * (27.0 * (e1 - e2) - new0),
                part(up_recv, 2, 1, j) - line(low_more, 6) * (27.0 * e2 - e1),
                part(up_recv, 2, 2, j) + line(low_more, 5) * e2,
                part(down_recv, 1, 0, j)
                - line(high_more, 0) * (du_high + 27.0 * (e8 - new7) + new6),
                part(down_recv, 1, 1, j) - line(high_more, 1) * (new7 - 27.0 * e8),
                part(down_recv, 1, 2, j) - line(high_more, 2) * e8,
            )
        )
        own_p0, own_p1, own_p7 = (row(p1, plane, i) for i in (0, 1, 7))
        d0, d6, d7 = changes(coef, low_p1, high_p1, high_p2)
        for i, d in ((0, d0), (6, d6), (7, d7)):
            add_row(w2, at + 2, i, d)
        du = -s_low * (27.0 * (low_w1 - rows_of(0, -1)) - (rows_of(0, 1) - rows_of(0, -2)))
        new1 = (
            low_w1
            - line(low_more, 1) * (27.0 * (own_p0 - low_p1) - (own_p1 - low_p2))
            - coef[12] * across(0)
        )
        new2 = (
            low_w2
            - line(low_more, 0) * (27.0 * (low_p1 - low_p2) - (own_p0 - low_p3))
            - coef[13] * across(1)
        )
        new8 = (
            high_w
            - line(high_more, 7) * (27.0 * (high_p2 - high_p1) - (high_p3 - own_p7))
            - coef[14] * across(2)
        )
        correct_pressure(p2, at, coef, du, d0, d6, d7, new1, new2, new8)
        return carry

    def first():
        lax.fori_loop(0, FIRST // H, functools.partial(correct_first, first_part), 0)

        @pl.when(first_r)
        def _():
            for ref in (u1, v1, w1, p1):
                zero(ref, 0, SHIFT * H)

        second_flows(-2, 5, 7)
        pl.when(first_r)(lambda: zero(u2, 0, 2 * H))
        second_pressures(0, 8, PART // 8)
        lax.fori_loop(0, PART // H, functools.partial(correct_second, first_pressure), 0)

    def last():
        lax.fori_loop(FIRST // H, ROWS // H, functools.partial(correct_first, last_part), 0)
        pl.when(last_r)(clear_after)
        second_flows(PART + 1, 8, 2)
        second_pressures(PART, 8, (N - PART) // 8)
        lax.fori_loop(PART // H, N // H, functools.partial(correct_second, last_pressure), 0)

    def correct_radial(j, carry):
        rows = halo[0, pl.ds(H * j + SHIFT - BASE, H), :]
        add_row(u2, H * j + 2, 0, -s_low * rows)
        return carry

    def radial(start, stop):
        lax.fori_loop(start // H, stop // H, correct_radial, 0)

    return Finish(first, last, radial)


def both_steps(
    ranges,
    heights,
    press_in,
    vert_in,
    radial_in,
    lateral_in,
    stiff_in,
    buoy_in,
    wind_in,
    p2,
    w2,
    u2,
    v2,
    p0,
    w0,
    p1,
    w1,
    u1,
    v1,
    up_last,
    down_last,
    low_w,
    halo,
    coef,
    low_more,
    high_more,
    u0,
    v0,
    stiff,
    buoy,
    wind,
    up_send,
    up_first,
    down_send,
    down_first,
    up_relay,
    down_relay,
    local_sem,
    send_sem,
    recv_sem,
    ready,
    via_ready,
):
    up_recv, down_recv = [*up_first, up_last], [*down_first, down_last]
    r, h = lax.axis_index("range"), lax.axis_index("height")
    first_r, last_r = r == 0, r == ranges - 1
    first_h, last_h = h == 0, h == heights - 1
    left = (lax.rem(r + ranges - 1, ranges), h)
    right = (lax.rem(r + 1, ranges), h)
    below = (r, lax.rem(h + heights - 1, heights))
    above = (r, lax.rem(h + 1, heights))
    no_left, no_right = jnp.logical_not(first_r), jnp.logical_not(last_r)
    no_below, no_above = jnp.logical_not(first_h), jnp.logical_not(last_h)
    odd = lax.rem(h, 2) == 1
    is_late = lax.rem(h // 2, 2) == 1
    is_early = jnp.logical_not(is_late)
    even = jnp.logical_not(odd)
    far_up, far_down = jnp.logical_and(odd, no_above), jnp.logical_and(even, no_below)
    near_up, near_down = jnp.logical_and(even, no_above), jnp.logical_and(odd, no_below)

    place = lax.rem(r, LINE)
    has_far = jnp.logical_or(far_up, far_down)
    goes_via = is_early & has_far & no_left & (place == LINE - 2)
    ends_via = is_late & has_far & no_left & (place == LINE - 2)
    relays = is_early & has_far & no_right & (place == LINE - 3)
    left_above, left_below = (left[0], above[1]), (left[0], below[1])
    right_above, right_below = (right[0], above[1]), (right[0], below[1])

    barrier = pltpu.get_barrier_semaphore()
    for there, device in (
        (no_right, right),
        (near_up, above),
        (near_down, below),
        (jnp.logical_and(is_early, far_up), above),
        (jnp.logical_and(is_early, far_down), below),
        (relays & far_up, right_above),
        (relays & far_down, right_below),
    ):

        @pl.when(there)
        def _():
            pl.semaphore_signal(barrier, inc=1, device_id=device, device_id_type=MESH)

    whole = pl.ds(0, N * H)
    loads = [
        pltpu.make_async_copy(src, dst, local_sem.at[i])
        for i, (src, dst) in enumerate(
            (
                (buoy_in, buoy),
                (stiff_in, stiff),
                (wind_in, wind),
                (press_in, p0.at[whole]),
                (vert_in, w0.at[whole]),
                (radial_in, u0.at[whole]),
                (lateral_in, v0.at[whole]),
            )
        )
    ]
    for load in loads:
        load.start()
    def remote(src, dst, i, device, sending=None):
        return pltpu.make_async_remote_copy(
            src_ref=src,
            dst_ref=dst,
            send_sem=send_sem.at[i if sending is None else sending],
            recv_sem=recv_sem.at[i],
            device_id=device,
            device_id_type=MESH,
        )

    tail = pl.ds(N * H, HALO * H)
    ups = [remote(up_send[i], up_recv[i], i, above) for i in range(3)]
    downs = [remote(down_send[i], down_recv[i], 3 + i, below) for i in range(3)]
    vias = (
        (far_up, remote(up_send[1], up_relay, 10, left)),
        (far_down, remote(down_send[1], down_relay, 10, left)),
    )
    forwards = (
        (far_up, remote(up_relay, up_recv[1], 1, right_above, 11)),
        (far_down, remote(down_relay, down_recv[1], 4, right_below, 11)),
    )
    lefts = [
        remote(src.at[pl.ds(0, count * H)], dst.at[pl.ds(N * H, count * H)], 6 + i, left)
        for i, (src, dst, count) in enumerate(
            (
                (press_in, p0, HALO),
                (radial_in, u0, HALO),
                (vert_in, w0, HALO - 1),
                (lateral_in, v0, HALO - 1),
            )
        )
    ]

    late_far = jnp.logical_and(is_late, jnp.logical_or(far_up, far_down))
    early_far = jnp.logical_and(is_early, jnp.logical_or(far_up, far_down))
    peers = sum(
        there.astype(jnp.int32)
        for there in (
            no_left,
            jnp.logical_or(near_up, near_down),
            late_far,
            ends_via,
        )
    )
    waits_long = jnp.logical_and(is_early, place == 0)

    def greet():
        pl.semaphore_wait(barrier, peers)
        for there, device, signal in (
            (is_late & far_up, above, ready),
            (is_late & far_down, below, ready),
            (ends_via & far_up, left_above, via_ready),
            (ends_via & far_down, left_below, via_ready),
        ):

            @pl.when(there)
            def _():
                pl.semaphore_signal(signal, inc=1, device_id=device, device_id_type=MESH)

        @pl.when(no_left)
        def _():
            for copy in lefts:
                copy.start()

    pl.when(jnp.logical_not(waits_long))(greet)

    for load in loads[:3]:
        load.wait()

    k = lax.broadcasted_iota(jnp.int32, (H, 128), 0)
    lane = lax.broadcasted_iota(jnp.int32, (H, 128), 1)
    spread_wind = jnp.broadcast_to(wind[...], (H, 128))
    top = heights * H - 1

    def wind_at(rows):
        chosen = jnp.where(lane == rows, spread_wind, 0.0)
        return jnp.broadcast_to(jnp.sum(chosen, axis=1, keepdims=True), (H, 128))

    def shear_at(rows):
        upper = wind_at(jnp.where(rows < top, rows + 1, top))
        lower = wind_at(jnp.where(rows > 0, rows - 1, 0))
        return 0.5 * (upper - lower)

    mine = k + h * H
    b24, c24 = buoy[...] * (1.0 / 24.0), stiff[...] * (1.0 / 24.0)
    a12 = wind_at(mine) * (1.0 / 12.0)
    half_shear = 0.5 * shear_at(mine)
    b27 = b24 * 27.0
    full = jnp.full((H, 128), 27.0, jnp.float32)
    one = jnp.full((H, 128), 1.0, jnp.float32)
    for i, value in enumerate(
        (
            b24,
            a12,
            half_shear,
            jnp.where(k > 0, half_shear, 0.0),
            b27,
            jnp.where(k < H - 1, b27, 0.0),
            jnp.where(k < H - 2, b24, 0.0),
            jnp.where(k > 0, b24, 0.0),
            c24,
            jnp.where(k > 0, full, 0.0),
            jnp.where(k > 1, one, 0.0),
            jnp.where(k < H - 1, one, 0.0),
        )
    ):
        coef[i] = value
    for i, outside in enumerate((-1, -2, H)):
        coef[12 + i] = wind_at(jnp.zeros_like(k) + (h * H + outside)) * (1.0 / 12.0)
    coef[15] = 0.5 * shear_at(jnp.zeros_like(k) + h * H)
    coef[16] = 0.5 * shear_at(jnp.zeros_like(k) + (h * H + H))

    def free_flows(start, step, times):
        def body(j, carry):
            at = start + step * j
            flows((p0, w0, u0, v0), (w1, u1, v1), at, step, at, coef)
            return carry

        lax.fori_loop(0, times, body, 0)

    def free_pressures(start, step, times):
        def body(j, carry):
            at = start + step * j
            pressures(p0, (w1, u1, v1), p1, at, at, step, at, coef)
            return carry

        lax.fori_loop(0, times, body, 0)

    up_rows = (
        ((p0, 7, 0), (w0, 7, 1)),
        ((w1, 7, 0), (w1, 6, 0)),
        ((p1, 7, 0), (p1, 6, 0), (p1, 5, 0)),
    )
    down_rows = (
        ((p0, 0, 0), (p0, 1, 0)),
        ((w1, 0, 0),),
        ((p1, 0, 0), (p1, 1, 0), (p1, 2, 0)),
    )

    def pack(buffer, to, rows, start, count):
        def body(j, carry):
            for q, (ref, height, later) in enumerate(rows):
                at = pl.ds(pl.multiple_of(to + q * count + j * H, H), H)
                buffer[at, :] = row(ref, start + later + H * j, height)
            return carry

        lax.fori_loop(0, count // H, body, 0)

    sides = (up_send, up_rows), (down_send, down_rows)

    def send(i):
        for there, copies in ((far_up, ups), (far_down, downs)):
            pl.when(is_late & there)(copies[i].start)
        if i == 1:
            for there, copy in vias:
                pl.when(there & goes_via)(copy.start)
        for there, copies in ((near_up, ups), (near_down, downs)):
            pl.when(there)(copies[i].start)

    for load in loads[3:]:
        load.wait()
    for buffers, (given, _, _) in sides:
        pack(buffers[0], 0, given, BASE, FIRST)
    first_w = line(w0, BASE * H + 7)
    for_above = jnp.where(k == 3, first_w, jnp.where(k > 3, c24, pltpu.roll(b24, 2, 0)))
    up_send[0][pl.ds(2 * FIRST, H), :] = for_above
    down_send[0][pl.ds(2 * FIRST, H), :] = jnp.where(k < 4, c24, pltpu.roll(b24, 7, 0))
    pl.when(jnp.logical_not(waits_long))(lambda: send(0))
    free_flows(BASE, 6, 7)
    free_pressures(BASE, 5, 8)
    for buffers, (_, flow_rows, press_rows) in sides:
        pack(buffers[1], 0, flow_rows, BASE, FIRST)
        pack(buffers[1], len(flow_rows) * FIRST, press_rows, SHIFT, PART)

    @pl.when(waits_long)
    def _():
        greet()
        send(0)

    send(1)

    eager = jnp.logical_and(is_early, place == LINE - 1)
    for there, outgoing in ((far_up, ups), (far_down, downs)):

        @pl.when(jnp.logical_and(there, eager))
        def _():
            pl.semaphore_wait(ready, 1)
            for copy in outgoing[:2]:
                copy.start()

    nothing = jnp.zeros((HALO * H, 128), jnp.float32)

    @pl.when(last_r)
    def _():
        for ref in (p0, u0, w0, v0):
            ref[tail, :] = nothing

    @pl.when(no_right)
    def _():
        for copy in lefts:
            copy.wait_recv()

    free_flows(45, 5, 3)

    def clear_after():
        for ref in (u1, v1, w1, p1):
            ref[pl.ds(N * H, 12 * H), :] = jnp.zeros((12 * H, 128), jnp.float32)

    pl.when(last_r)(clear_after)
    free_pressures(43, 4, 4)
    pl.when(last_r)(clear_after)
    for buffers, (given, flow_rows, press_rows) in sides:
        pack(buffers[2], 0, given + flow_rows, BASE + FIRST, REST)
        pack(buffers[2], len(given + flow_rows) * REST, press_rows, SHIFT + PART, REST)
    send(2)

    for there, outgoing in ((far_up, ups), (far_down, downs)):
        pl.when(jnp.logical_and(there, eager))(outgoing[2].start)

        @pl.when(jnp.logical_and(there, jnp.logical_and(is_early, jnp.logical_not(eager))))
        def _():
            pl.semaphore_wait(ready, 1)
            outgoing[0].start()
            pl.when(jnp.logical_not(goes_via))(outgoing[1].start)
            outgoing[2].start()

    pl.when(relays)(lambda: pl.semaphore_wait(via_ready, 1))
    for (there, came), (_, copy) in zip(vias, forwards):

        @pl.when(there & relays)
        def _():
            came.wait_recv()
            copy.start()

    def arrived(parts):
        for none, some, copies, buffers in (
            (first_h, no_below, ups, up_recv),
            (last_h, no_above, downs, down_recv),
        ):

            @pl.when(some)
            def _():
                for i in parts:
                    copies[i].wait_recv()

            @pl.when(none)
            def _():
                for i in parts:
                    zero(buffers[i], 0, buffers[i].shape[0])

    finish = finishing(
        ranges, p0, w0, p1, w1, u1, v1, p2, w2, u2, v2, up_recv, down_recv, low_w, halo, coef, low_more, high_more
    )

    arrived((0, 1))
    more = pl.ds(2 * FIRST, H)
    low_more[...], high_more[...] = up_recv[0][more, :], down_recv[0][more, :]
    zero(low_w, 0, H)
    low_w[pl.ds(H, 1), :] = low_more[pl.ds(3, 1), :]
    low_w[pl.ds(H + 1, FIRST), :] = up_recv[0][pl.ds(FIRST, FIRST), :]
    finish.first()

    arrived((2,))
    low_w[pl.ds(H + 1 + FIRST, REST), :] = up_recv[2][pl.ds(REST, REST), :]
    for some, far, copies in ((no_above, far_up, ups), (no_below, far_down, downs)):

        @pl.when(some)
        def _():
            copies[0].wait_send()
            pl.when(jnp.logical_not(far & goes_via))(copies[1].wait_send)
            copies[2].wait_send()

    for there, copy in vias:
        pl.when(there & goes_via)(copy.wait_send)
    for there, copy in forwards:
        pl.when(there & relays)(copy.wait_send)

    @pl.when(no_left)
    def _():
        for copy in lefts:
            copy.wait_send()


def store(ranges, refs):
    p2, w2, u2, v2, p0, w0, p1, w1, u1, v1, up_last, down_last, *rest = refs
    low_w, halo, coef, low_more, high_more, press, vert, radial, lateral, sems = rest
    finish = finishing(
        ranges, p0, w0, p1, w1, u1, v1, p2, w2, u2, v2,
        (None, None, up_last), (None, None, down_last), low_w, halo, coef, low_more, high_more,
    )

    def copy(i, src, early, dst, start, count):
        from_rows, to_rows = pl.ds((start + early) * H, count * H), pl.ds(start * H, count * H)
        return pltpu.make_async_copy(src.at[from_rows], dst.at[to_rows], sems.at[i])

    done = PART - H
    finish.radial(0, done)
    fields = (v2, 2, lateral), (w2, 2, vert), (p2, 0, press)
    copies = [copy(i, *field, 0, PART) for i, field in enumerate(fields)]
    copies.append(copy(6, u2, 2, radial, 0, done))
    for one in copies:
        one.start()
    finish.last()
    others = [copy(3 + i, *field, PART, N - PART) for i, field in enumerate(fields)]
    for one in others:
        one.start()
    finish.radial(done, N)
    others.append(copy(7, u2, 2, radial, done, N - done))
    others[-1].start()
    for one in copies + others:
        one.wait()


def solution(mesh):
    ranges, heights = mesh.shape["range"], mesh.shape["height"]

    def on_device(press, vert, radial, lateral, stiff, buoy, wind):
        def field(count):
            return pltpu.VMEM((count * H, 128), jnp.float32)

        def messages(rows, press_rows):
            flow_rows = rows - 2 - press_rows
            first = 2 * FIRST + H
            second = flow_rows * FIRST + press_rows * PART
            third = rows * REST
            return [pltpu.VMEM((count, 128), jnp.float32) for count in (first, second, third)]

        flat = [x.reshape(N * H, 128) for x in (press, vert, radial, lateral)]
        arguments = [
            pltpu.with_memory_space_constraint(x, pltpu.HBM)
            for x in (*flat, stiff, buoy, wind.reshape(1, 128))
        ]
        result = [field(N), field(N + 4), field(N + 4), field(N + 4)] + [field(64)] * 6
        result += [
            messages(UP, 3)[2],
            messages(DOWN, 3)[2],
            pltpu.VMEM((ROWS + 2 * H, 128), jnp.float32),
            pltpu.VMEM((3, ROWS, 128), jnp.float32),
            pltpu.VMEM((17, H, 128), jnp.float32),
            field(1),
            field(1),
        ]
        state = pl.pallas_call(
            lambda *refs: both_steps(ranges, heights, *refs),
            out_shape=result,
            in_specs=[pl.BlockSpec(memory_space=pltpu.HBM)] * 7,
            out_specs=[pl.BlockSpec(memory_space=pltpu.VMEM)] * len(result),
            scratch_shapes=[field(64)] * 2
            + [
                field(1),
                field(1),
                pltpu.VMEM((1, 128), jnp.float32),
                messages(UP, 3),
                messages(UP, 3)[:2],
                messages(DOWN, 3),
                messages(DOWN, 3)[:2],
                messages(UP, 3)[1],
                messages(DOWN, 3)[1],
                pltpu.SemaphoreType.DMA((7,)),
                pltpu.SemaphoreType.DMA((12,)),
                pltpu.SemaphoreType.DMA((11,)),
                pltpu.SemaphoreType.REGULAR,
                pltpu.SemaphoreType.REGULAR,
            ],
            compiler_params=pltpu.CompilerParams(
                collective_id=0, has_side_effects=True, vmem_limit_bytes=24 * 2**20
            ),
        )(*arguments)
        out = pl.pallas_call(
            lambda *refs: store(ranges, refs),
            out_shape=[jax.ShapeDtypeStruct((N * H, 128), jnp.float32)] * 4,
            in_specs=[pl.BlockSpec(memory_space=pltpu.VMEM)] * len(result),
            out_specs=[pl.BlockSpec(memory_space=pltpu.HBM)] * 4,
            scratch_shapes=[pltpu.SemaphoreType.DMA((8,))],
            compiler_params=pltpu.CompilerParams(vmem_limit_bytes=24 * 2**20),
        )(*state)
        return tuple(x.reshape(N, H, 128) for x in out)

    field_spec = P("range", "height", None)
    return jax.shard_map(
        on_device,
        mesh=mesh,
        in_specs=(field_spec,) * 4 + (P("height", None), P("height", None), P()),
        out_specs=(field_spec,) * 4,
        check_vma=False,
    )
```
